32 devices in a mesh: dp: 4 (over z), seq: 8 (over y, x, core).
Axes of the slice: x: 2, y: 2, z: 4, core: 2. Of those that a mesh axis runs over, the one named last changes fastest.
Arguments:
- inputs: bfloat16 [4, 1024, 4096], P('dp', 'seq'), may hold values from -6 to 6
- out_grads: bfloat16 [4, 1024, 14336], P('dp', 'seq'), may hold values from -6 to 6
- valid: int32 [4, 1024], P('dp', 'seq'), may hold values 0 or 1
- doc_blocks: int32 [4, 4], P('dp'), may hold values from 1 to 4, 8 in all within a row
- doc_ids: int32 [16], replicated, may hold values from 0 to 15, each once
- proj_in: bfloat16 [4096, 64], P('seq'), may hold values from -0.09375 to 0.09375
- proj_out: bfloat16 [14336, 64], P('seq'), may hold values from -0.046875 to 0.046875
- test_grads: bfloat16 [256, 4096], P('seq'), may hold values from -192 to 192
Outputs:
- scores: float32 [16, 256], P(None, 'seq')
The draws below stay inside these ranges and needn't reach their ends.
Inputs may be any that keep to these rules, and one draw needn't show every extreme that they name: `doc_blocks`: each group's lengths sum to 8; the largest is 4 in every group. `doc_ids`: every document number appears once.
All inputs are finite; a program needn't handle non-finite values. No bound on the sum of `valid` on one device may be relied on, other than what follows from the above.
Results may differ from the reference program's by a relative error of at most 0.0003.
Values may be sent and summed in bfloat16 or wider, within the bound.
No kernel may reach another device: no remote copies, remote signals or barrier semaphores. Data moves between devices by JAX's collectives and lax.ppermute only.
A program may use at most 64 MiB of HBM per device.

```python
import math
import jax
import jax.numpy as jnp
import numpy as np
from jax import lax

D = 4096
FF = 14336
PROJ_IN = 64
PROJ_OUT = 64
FEAT = 4096
BLOCK = 128
DOC_GRP = 4
GROUPS = 4
SEQ_TOK = 1024
BLK_GRP = 8
MOST = 4
NDOCS = 16
NTEST = 256


def touch_ends(values, key, least, top_value):
    extent = values.shape
    index_at = [jax.random.randint(jax.random.fold_in(key, axis), (), 0, extent[axis]) for axis in range(len(extent))]
    values = values.at[tuple(index_at)].set(least)
    longest = extent.index(max(extent))
    index_at[longest] = (index_at[longest] + 1) % extent[longest]
    return values.at[tuple(index_at)].set(top_value)


def block_scale(key, shape, split, smallest, top_value):
    gain = 1.0
    for position, shards_of in split:
        heights = jax.random.uniform(jax.random.fold_in(jax.random.fold_in(key, 6), position), (shards_of,), jnp.float32, smallest / len(split), top_value / len(split))
        gain = gain * jnp.repeat(jnp.exp(heights), shape[position] // shards_of).reshape((-1,) + (1,) * (len(shape) - 1 - position))
    return gain


def profile(amount, total, most, slope):
    portions = [(1 << 20) // math.isqrt(grade ** slope) + 1 for grade in range(2, amount + 1)]
    surplus, holding = total - most - (amount - 1), [1] * (amount - 1)
    while surplus > 0:
        free = [i for i in range(amount - 1) if holding[i] < most]
        mass, budget = sum([portions[i] for i in free]), surplus
        for i in free:
            more = min(most - holding[i], max(1, budget * portions[i] // mass), surplus)
            holding[i] = holding[i] + more
            surplus = surplus - more
    return np.array([most] + holding)


def uneven_parts(own_key, amount, total, reach, lean):
    if amount == 2:
        one = jax.random.randint(own_key, (), max(1, total - reach), min(reach, total - 1) + 1)
        return jnp.stack([one, total - one])
    sizes = jnp.asarray(profile(amount, total, reach, lean), jnp.int32)
    pairs = (amount - 1) // 2
    giver, receiver = sizes[1:1 + 2 * pairs:2], sizes[2:2 + 2 * pairs:2]
    margin = jnp.minimum(giver - 1, reach - receiver)
    moved = jax.random.randint(jax.random.fold_in(own_key, 1), (pairs,), 0, 1 << 20) % (margin + 1)
    sizes = sizes.at[1:1 + 2 * pairs:2].set(giver - moved).at[2:2 + 2 * pairs:2].set(receiver + moved)
    return sizes[jax.random.permutation(jax.random.fold_in(own_key, 2), amount)]


def normal_values(rng, dims, spread, reach, split=(), kind=jnp.bfloat16):
    array = jax.random.normal(rng, dims, jnp.float32) * spread
    if len(split) > 0:
        array = block_scale(rng, dims, split, -0.22, 0.18) * array
    return jnp.clip(array, min=-reach, max=reach).astype(kind)


def setup_inputs(seed: int = 0) -> dict:
    key_of = jax.random.split(jax.random.key(seed), 9)
    return {
        "inputs": normal_values(key_of[0], (GROUPS, SEQ_TOK, D), 1.0, 6.0, ((0, 4), (1, 8))),
        "out_grads": normal_values(key_of[1], (GROUPS, SEQ_TOK, FF), 1.0, 6.0, ((0, 4), (1, 8))),
        "valid": touch_ends((jax.random.randint(key_of[2], (GROUPS, SEQ_TOK), 0, 8) < 7).astype(jnp.int32), jax.random.fold_in(key_of[2], 1), 0, 1),
        "doc_blocks": jax.vmap(lambda own: uneven_parts(own, DOC_GRP, BLK_GRP, MOST, 2))(jax.random.split(key_of[3], GROUPS)).reshape((GROUPS, DOC_GRP)).astype(jnp.int32),
        "doc_ids": jax.random.permutation(key_of[4], NDOCS).astype(jnp.int32),
        "proj_in": normal_values(key_of[5], (D, PROJ_IN), D ** -0.5, 0.09375, ((0, 8),)),
        "proj_out": normal_values(key_of[6], (FF, PROJ_OUT), FF ** -0.5, 0.046875, ((0, 8),)),
        "test_grads": normal_values(key_of[7], (NTEST, FEAT), 32.0, 192.0, ((0, 8),)),
    }


def group_grads(args, proj_in, proj_out):
    inputs, out_grads, valid, blocks = args
    px = jnp.dot(inputs.astype(jnp.float32), proj_in.astype(jnp.float32), preferred_element_type=jnp.float32)
    pg = jnp.dot(out_grads.astype(jnp.float32), proj_out.astype(jnp.float32), preferred_element_type=jnp.float32)
    ends = jnp.cumsum(blocks).astype(jnp.int32)
    blk = (jnp.arange(SEQ_TOK, dtype=jnp.int32) // BLOCK).astype(jnp.int32)
    owner = jnp.sum((blk[:, None] >= ends[None, :]).astype(jnp.int32), axis=1)
    onehot = ((owner[:, None] == jnp.arange(DOC_GRP, dtype=jnp.int32)[None, :]) & (valid[:, None] == 1)).astype(jnp.float32)
    weighted = (onehot[:, :, None] * pg[:, None, :]).reshape(SEQ_TOK, DOC_GRP * PROJ_OUT)
    summed = jnp.dot(weighted.T, px, precision=lax.Precision.HIGHEST)
    return summed.reshape(DOC_GRP, FEAT)

def reference(inputs, out_grads, valid, doc_blocks, doc_ids, proj_in, proj_out, test_grads):
    per_group = lax.map(lambda a: group_grads(a, proj_in, proj_out), (inputs, out_grads, valid, doc_blocks))
    doc_grads = per_group.reshape(NDOCS, FEAT)
    gram = jnp.dot(doc_grads, doc_grads.T, precision=lax.Precision.HIGHEST)
    damp = 0.1 * jnp.trace(gram) / NDOCS
    cross = jnp.dot(doc_grads, test_grads.astype(jnp.float32).T, precision=lax.Precision.HIGHEST)
    matrix = gram / NDOCS + damp * jnp.eye(NDOCS, dtype=jnp.float32)
    factor = jnp.linalg.cholesky(matrix)
    middle = lax.linalg.triangular_solve(factor, cross, left_side=True, lower=True)
    solved = lax.linalg.triangular_solve(factor, middle, left_side=True, lower=True, transpose_a=True)
    placing = (doc_ids[None, :] == jnp.arange(NDOCS, dtype=jnp.int32)[:, None]).astype(jnp.float32)
    return jnp.dot(placing, solved, precision=lax.Precision.HIGHEST)
```

```python
import jax
import jax.numpy as jnp
from jax import lax
from jax.sharding import PartitionSpec as P

BLOCK = 128
HIGH = lax.Precision.HIGHEST


def owner_weights(doc_blocks, valid, slots):
    ends = jnp.cumsum(doc_blocks[0])
    position = lax.axis_index("seq") * slots + jnp.arange(slots, dtype=jnp.int32)
    owner = jnp.sum((position // BLOCK)[:, None] >= ends[None, :], axis=1)
    mine = owner[None, :] == jnp.arange(ends.shape[0])[:, None]
    return (mine & (valid[0][None, :] == 1)).astype(jnp.float32)


def solve_and_place(gram, cross, doc_ids):
    ndocs = gram.shape[0]
    damp = 0.1 * jnp.trace(gram) / ndocs
    matrix = gram / ndocs + damp * jnp.eye(ndocs, dtype=jnp.float32)
    factor = jnp.linalg.cholesky(matrix)
    middle = lax.linalg.triangular_solve(factor, cross, left_side=True, lower=True)
    solved = lax.linalg.triangular_solve(
        factor, middle, left_side=True, lower=True, transpose_a=True
    )
    placing = (doc_ids[None, :] == jnp.arange(ndocs, dtype=jnp.int32)[:, None]).astype(jnp.float32)
    return jnp.dot(placing, solved, precision=HIGH)


def any_mesh(inputs, out_grads, valid, doc_blocks, doc_ids, proj_in, proj_out, test_grads):
    px = jnp.dot(inputs[0], lax.all_gather(proj_in, "seq", tiled=True), preferred_element_type=jnp.float32)
    pg = jnp.dot(out_grads[0], lax.all_gather(proj_out, "seq", tiled=True), preferred_element_type=jnp.float32)
    weights = owner_weights(doc_blocks, valid, px.shape[0])
    weighted = weights[:, None, :] * pg.T[None, :, :]
    grads = jnp.einsum("jat,tb->jab", weighted, px, precision=HIGH)
    grads = lax.psum(grads.reshape(grads.shape[0], -1), "seq")
    grads = lax.all_gather(grads, "dp", tiled=True)
    gram = jnp.dot(grads, grads.T, precision=HIGH)
    cross = jnp.dot(grads, test_grads.astype(jnp.float32).T, precision=HIGH)
    return solve_and_place(gram, cross, doc_ids)


def paired_chips(inputs, out_grads, valid, doc_blocks, doc_ids, proj_in, proj_out, test_grads):
    seq = lax.axis_index("seq")
    dp = lax.axis_index("dp")
    core = seq & 1

    def swap(x, bits):
        return lax.ppermute(x, "seq", [(i, i ^ b) for i, b in enumerate(bits)])

    first, second, other = (2, 4) * 4, (4, 2) * 4, (1,) * 8

    def gather(own):
        a = swap(own, first)
        b = swap(own, second)
        c = swap(a, second)
        near = [own, a, b, c]
        far = [swap(x, other) for x in near]
        return near, far

    def project(tokens, own):
        near, far = gather(own)
        rows = own.shape[0]
        one = 2 + 2 * core
        two = 6 - one
        ids = [seq, seq ^ one, seq ^ two, seq ^ 6]
        far_ids = [seq ^ 1, seq ^ 1 ^ two, seq ^ 1 ^ one, seq ^ 7]
        total = 0.0
        for i, w in zip(ids + far_ids, near + far):
            part = lax.dynamic_slice(tokens, (0, i * rows), (tokens.shape[0], rows))
            total = total + jnp.dot(part, w, preferred_element_type=jnp.float32)
        return total

    pg = project(out_grads[0], proj_out)
    px = project(inputs[0], proj_in)
    weights = owner_weights(doc_blocks, valid, px.shape[0])
    weighted = weights[:, None, :] * pg.T[None, :, :]
    grads = jnp.einsum("jat,tb->jab", weighted, px, precision=HIGH)
    docs, aa, bb = grads.shape
    halves = grads.reshape(docs, 2, aa // 2, bb)
    keep = lax.dynamic_index_in_dim(halves, core, 1, keepdims=False)
    send = lax.dynamic_index_in_dim(halves, 1 - core, 1, keepdims=False)
    mine = keep + swap(send, other)
    mine = (mine + swap(mine, (6,) * 8)) + (swap(mine, (2,) * 8) + swap(mine, (4,) * 8))
    ndp = lax.axis_size("dp")
    every = [mine] + [lax.ppermute(mine, "dp", [(i, i ^ k) for i in range(ndp)]) for k in range(1, ndp)]
    allg = jnp.zeros((ndp,) + mine.shape, jnp.float32)
    for k, m in enumerate(every):
        allg = lax.dynamic_update_slice(allg, m[None], (dp ^ k, 0, 0, 0))
    allg = allg.reshape(ndp * docs, -1)
    ntest, feat = test_grads.shape
    th = test_grads.reshape(ntest, 2, feat // 2)
    t_keep = lax.dynamic_index_in_dim(th, core, 1, keepdims=False)
    t_send = lax.dynamic_index_in_dim(th, 1 - core, 1, keepdims=False)
    t_recv = swap(t_send, other)
    gram = jnp.dot(allg, allg.T, precision=HIGH)
    cross = jnp.dot(allg, t_keep.astype(jnp.float32).T, precision=HIGH)
    far = jnp.dot(allg, t_recv.astype(jnp.float32).T, precision=HIGH)
    got = swap(jnp.concatenate([far, gram], axis=1), other)
    cross = cross + got[:, :ntest]
    gram = gram + got[:, ntest:]
    return solve_and_place(gram, cross, doc_ids)


def solution(mesh):
    in_specs = (
        P("dp", "seq", None),
        P("dp", "seq", None),
        P("dp", "seq"),
        P("dp", None),
        P(),
        P("seq", None),
        P("seq", None),
        P("seq", None),
    )
    fast = mesh.shape["seq"] == 8 and mesh.shape["dp"] == 4
    return jax.shard_map(
        paired_chips if fast else any_mesh,
        mesh=mesh, in_specs=in_specs, out_specs=P(None, "seq"), check_vma=False,
    )
```

```python
import functools

import jax
import jax.numpy as jnp
from jax import lax
from jax.experimental import pallas as pl
from jax.experimental.pallas import tpu as pltpu
from jax.sharding import PartitionSpec as P

BLOCK = 128
HIGH = lax.Precision.HIGHEST
F32 = jnp.float32
VMEM = pltpu.VMEM
LIMIT = 16 * 1024 * 1024


def any_mesh(inputs, out_grads, valid, doc_blocks, doc_ids, proj_in, proj_out, test_grads):
    px = jnp.dot(inputs[0], lax.all_gather(proj_in, "seq", tiled=True), preferred_element_type=F32)
    pg = jnp.dot(out_grads[0], lax.all_gather(proj_out, "seq", tiled=True), preferred_element_type=F32)
    slots = px.shape[0]
    ends = jnp.cumsum(doc_blocks[0])
    position = lax.axis_index("seq") * slots + jnp.arange(slots, dtype=jnp.int32)
    owner = jnp.sum((position // BLOCK)[:, None] >= ends[None, :], axis=1)
    mine = owner[None, :] == jnp.arange(ends.shape[0])[:, None]
    weights = (mine & (valid[0][None, :] == 1)).astype(F32)
    weighted = weights[:, None, :] * pg.T[None, :, :]
    grads = jnp.einsum("jat,tb->jab", weighted, px, precision=HIGH)
    grads = lax.psum(grads.reshape(grads.shape[0], -1), "seq")
    grads = lax.all_gather(grads, "dp", tiled=True)
    gram = jnp.dot(grads, grads.T, precision=HIGH)
    cross = jnp.dot(grads, test_grads.astype(F32).T, precision=HIGH)
    ndocs = gram.shape[0]
    damp = 0.1 * jnp.trace(gram) / ndocs
    factor = jnp.linalg.cholesky(gram / ndocs + damp * jnp.eye(ndocs, dtype=F32))
    middle = lax.linalg.triangular_solve(factor, cross, left_side=True, lower=True)
    solved = lax.linalg.triangular_solve(factor, middle, left_side=True, lower=True, transpose_a=True)
    placing = (doc_ids[None, :] == jnp.arange(ndocs, dtype=jnp.int32)[:, None]).astype(F32)
    return jnp.dot(placing, solved, precision=HIGH)


def place(seq, dp):
    bits = seq ^ (seq >> 1) ^ (seq >> 2) ^ dp ^ (dp >> 1)
    return bits & 1


def here():
    seq, dp = lax.axis_index("seq"), lax.axis_index("dp")
    return seq, dp, place(seq, dp)


def in_vmem(*arrays):
    return [pltpu.with_memory_space_constraint(x, VMEM) for x in arrays]


def vmem_call(body, outs, args, hbm=(), scratch=(), name=None, moved=0):
    specs = [pl.BlockSpec(memory_space=VMEM)] * len(args) + [pl.BlockSpec(memory_space=pltpu.HBM)] * len(hbm)
    far = [pltpu.with_memory_space_constraint(x, pltpu.HBM) for x in hbm]
    return pl.pallas_call(
        body,
        out_shape=[VMEM(s, d) for s, d in outs],
        in_specs=specs,
        out_specs=[pl.BlockSpec(memory_space=VMEM)] * len(outs),
        scratch_shapes=list(scratch),
        name=name,
        compiler_params=pltpu.CompilerParams(vmem_limit_bytes=LIMIT),
        cost_estimate=pl.CostEstimate(flops=0, transcendentals=0, bytes_accessed=moved),
    )(*in_vmem(*args), *far)


def source(seq, slot):
    even, odd = ((0, 0), (5, 3), (3, 5), (6, 6))[slot]
    return seq ^ jnp.where(seq & 1 == 0, even, odd)


def weights_body(valid, blocks, out_t, in_t, first, second, weights, valid_v, blocks_s, sems):
    seq, _, _ = here()
    rows_out, rows_in, size = out_t.shape[1], in_t.shape[1], first.shape[1]
    rest = rows_out - size
    copies = [
        pltpu.make_async_copy(out_t.at[:, pl.ds(0, size)], first, sems.at[0]),
        pltpu.make_async_copy(out_t.at[:, pl.ds(size, rest)], second.at[:, pl.ds(0, rest)], sems.at[1]),
        pltpu.make_async_copy(in_t, second.at[:, pl.ds(rest, rows_in)], sems.at[2]),
        pltpu.make_async_copy(valid, valid_v, sems.at[3]),
        pltpu.make_async_copy(blocks, blocks_s, sems.at[4]),
    ]
    for c in copies:
        c.start()
    for c in copies:
        c.wait()
    slots = valid.shape[1]
    blk = (seq * slots + lax.broadcasted_iota(jnp.int32, weights.shape, 1)) // BLOCK
    row = lax.broadcasted_iota(jnp.int32, weights.shape, 0)
    owner = jnp.zeros_like(blk)
    end = 0
    for j in range(blocks.shape[1]):
        end = end + blocks_s[0, j]
        owner = owner + (blk >= end).astype(jnp.int32)
    weights[...] = jnp.where((owner == row) & (valid_v[...] == 1), 1.0, 0.0)


def column_copies(og, inp, out, mine, sems):
    nseq = lax.axis_size("seq")
    wo, wi = og.shape[1] // nseq, inp.shape[1] // nseq
    copies = []
    for k in range(4):
        shard = source(mine, k)
        base = k * (wo + wi)
        copies.append(pltpu.make_async_copy(
            og.at[:, pl.ds(pl.multiple_of(shard * wo, wo), wo)], out.at[:, pl.ds(base, wo)], sems.at[2 * k]))
        copies.append(pltpu.make_async_copy(
            inp.at[:, pl.ds(pl.multiple_of(shard * wi, wi), wi)], out.at[:, pl.ds(base + wo, wi)], sems.at[2 * k + 1]))
    return copies


def send_body(_, og, inp, send, sems):
    seq, _, _ = here()
    copies = column_copies(og, inp, send, seq ^ 1, sems)
    for c in copies:
        c.start()
    for c in copies:
        c.wait()


def keep_body(_, og, inp, tests, ids, keep, t_own, t_far, rows, ids_s, sems):
    seq, _, half = here()
    hf = t_own.shape[1]
    copies = column_copies(og, inp, keep, seq, sems)
    copies.append(pltpu.make_async_copy(tests.at[:, pl.ds(pl.multiple_of(half * hf, hf), hf)], t_own, sems.at[8]))
    copies.append(pltpu.make_async_copy(tests.at[:, pl.ds(pl.multiple_of((1 - half) * hf, hf), hf)], t_far, sems.at[9]))
    copies.append(pltpu.make_async_copy(ids, ids_s, sems.at[10]))
    for c in copies:
        c.start()
    for c in copies:
        c.wait()
    for r in range(rows.shape[0]):
        rows[r:r + 1, :] = jnp.full((1, rows.shape[1]), ids_s[r], jnp.int32)


def nt(a, b, precision=None):
    return lax.dot_general(a, b, (((1,), (1,)), ((), ())), precision=precision, preferred_element_type=F32)


def project(w, near, far, base):
    cols = pl.ds(base, w.shape[1])
    return nt(w, jnp.concatenate([near[:, cols], far[:, cols]], axis=0))


def near_body(w1, w2, a1, a2, b1, b2, near, far, pg, px, *, wi):
    size = w1.shape[1]
    rest = w2.shape[1] - wi
    total, total_x = 0.0, 0.0
    for k, (x, y) in enumerate(((w1, w2), (a1, a2), (b1, b2))):
        base = k * (size + rest + wi)
        total = total + project(x[...], near, far, base)
        total = total + project(y[:, :rest], near, far, base + size)
        total_x = total_x + project(y[:, rest:], near, far, base + size + rest)
    pg[...] = total
    px[...] = total_x


def diagonal_body(c1, pg_in, near, far, pg):
    base = near.shape[1] // 4 * 3
    pg[...] = pg_in[...] + project(c1[...], near, far, base)


def last_body(c2, pg_in, px_in, near, far, out, *, wi):
    base = near.shape[1] - c2.shape[1]
    rest = c2.shape[1] - wi
    rows = pg_in.shape[0]
    out[:rows] = pg_in[...] + project(c2[:, :rest], near, far, base)
    out[rows:2 * rows] = px_in[...] + project(c2[:, rest:], near, far, base + rest)


def grads_body(mine, far, weights, weights2, grads, pgs):
    _, _, half = here()
    slots = pgs.shape[2]
    rows = mine.shape[0] // 2
    hw = rows // 2
    pairs = hw // 2
    docs = grads.shape[0] // pairs
    both = []
    for base in (0, rows):
        block = pl.ds(base, rows)
        both.append([mine[block, :slots] + far[block, slots:], mine[block, slots:] + far[block, :slots]])
    for u in range(2):
        pgs[u] = jnp.where(half == 1, both[0][u][hw:], both[0][u][:hw])
    px = jnp.concatenate(both[1], axis=1)
    tokens = jnp.concatenate([weights[...], weights2[...]], axis=1)
    parts = []
    for q in range(2):
        some = jnp.concatenate([pgs[u, pl.ds(q, pairs, stride=2), :] for u in range(2)], axis=1)
        weighted = jnp.concatenate([some * tokens[j:j + 1, :] for j in range(docs)], axis=0)
        parts.append(nt(weighted, px, HIGH))
    grads[...] = jnp.concatenate(parts, axis=1)


def products_body(m0, m1, m2, m3, t_own, t_far, out, every):
    seq, dp, _ = here()
    rows = m0.shape[0]
    for k, m in enumerate((m0, m1, m2, m3)):
        every[pl.ds(pl.multiple_of((dp ^ k) * rows, rows), rows), :] = m[...]
    docs = out.shape[0]
    pairs = every.shape[0] // docs
    flat = jnp.concatenate([every[pl.ds(i, docs, stride=pairs), :] for i in range(pairs)], axis=1)
    gram = nt(flat, flat, HIGH)
    own, far = t_own[...], t_far[...]
    core = seq & 1
    tests = jnp.concatenate([jnp.where(core == 0, own, far), jnp.where(core == 0, far, own)], axis=0)
    high = flat.astype(jnp.bfloat16)
    rest = flat - high.astype(F32)
    mid = rest.astype(jnp.bfloat16)
    low = (rest - mid.astype(F32)).astype(jnp.bfloat16)
    cross = nt(low, tests) + nt(mid, tests) + nt(high, tests)
    pad = jnp.zeros((docs, out.shape[1] - cross.shape[1] - docs), F32)
    out[...] = jnp.concatenate([cross, gram, pad], axis=1)


def solve_body(mine, far, rows, out):
    docs, tests = out.shape
    seq, _, _ = here()
    both = mine[...] + far[...]
    shape = both.shape
    row = lax.broadcasted_iota(jnp.int32, shape, 0)
    columns = [jnp.broadcast_to(both[:, 2 * tests + k:2 * tests + k + 1], shape) for k in range(docs)]
    trace = columns[0][0:1, :]
    for k in range(1, docs):
        trace = trace + columns[k][k:k + 1, :]
    damp = 0.1 * trace / docs
    columns = [c / docs + jnp.where(row == k, damp, 0.0) for k, c in enumerate(columns)]
    scale = jnp.zeros(shape, F32)
    for k in range(docs):
        inverse = 1.0 / columns[k][k:k + 1, :]
        scale = jnp.where(row == k, inverse, scale)
        factor = jnp.where(row == k, 0.0, columns[k] * inverse)
        both = both - factor * both[k:k + 1, :]
        for j in range(k + 1, docs):
            columns[j] = columns[j] - factor * columns[j][k:k + 1, :]
    solved = both * scale
    placed = jnp.zeros(shape, F32)
    for r in range(docs):
        placed = jnp.where(row == rows[r:r + 1, :], solved[r:r + 1, :], placed)
    out[...] = jnp.where(seq & 1 == 0, placed[:, :tests], placed[:, tests:2 * tests])


def paired_chips(inputs, out_grads, valid, doc_blocks, doc_ids, proj_in, proj_out, test_grads):
    ndp, nseq = lax.axis_size("dp"), lax.axis_size("seq")
    docs = doc_blocks.shape[1]
    ndocs = docs * ndp
    inp, og = inputs[0], out_grads[0]
    width = proj_out.shape[1]
    hw = width // 2
    wo, wi = proj_out.shape[0], proj_in.shape[0]
    slots = og.shape[0]
    ntest, feat = test_grads.shape
    bf = jnp.bfloat16

    def move(x, to):
        pairs = [(z * nseq + s, (lambda t: t[0] * nseq + t[1])(to(z, s))) for z in range(ndp) for s in range(nseq)]
        return lax.ppermute(x, ("dp", "seq"), pairs)

    def swap(x):
        return move(x, lambda z, s: (z, s ^ 1))

    def ring(x, step):
        return move(x, lambda z, s: (z, s ^ ((3, 5)[(s & 1) ^ step])))

    size = (wo + wi) // 256 * 128
    first, second, weights = vmem_call(
        weights_body,
        [((width, size), bf), ((width, wo + wi - size), bf), ((8, slots), F32)],
        [], hbm=[valid, doc_blocks, proj_out.T, proj_in.T],
        scratch=[VMEM((1, slots), jnp.int32), pltpu.SMEM((1, docs), jnp.int32), pltpu.SemaphoreType.DMA((5,))],
        name="weights",
    )
    a1, b1 = ring(first, 0), ring(first, 1)
    a2, b2 = ring(second, 0), ring(second, 1)
    weights2 = swap(weights)
    (tokens,) = vmem_call(
        send_body, [((slots, 4 * (wo + wi)), bf)], [weights], hbm=[og, inp],
        scratch=[pltpu.SemaphoreType.DMA((8,))], name="send", moved=1 * slots * (wo + wi) * 16,
    )
    far = swap(tokens)
    near, t_own, t_send, rows = vmem_call(
        keep_body, [((slots, 4 * (wo + wi)), bf)] + [((ntest, feat // 2), bf)] * 2 + [((ndocs, -(-(2 * ntest + ndocs) // 128) * 128), jnp.int32)],
        [tokens], hbm=[og, inp, test_grads, doc_ids],
        scratch=[pltpu.SMEM((ndocs,), jnp.int32), pltpu.SemaphoreType.DMA((11,))], name="keep", moved=1 * slots * (wo + wi) * 16,
    )
    t_far = swap(t_send)
    c1 = ring(a1, 0)
    c2 = ring(a2, 0)
    part = ((width, 2 * slots), F32)
    pg, px = vmem_call(
        functools.partial(near_body, wi=wi), [part, part],
        [first, second, a1, a2, b1, b2, near, far], name="near",
    )
    (pg,) = vmem_call(diagonal_body, [part], [c1, pg, near, far], name="diagonal")
    (mine,) = vmem_call(
        functools.partial(last_body, wi=wi), [((2 * width, 2 * slots), F32)],
        [c2, pg, px, near, far], name="last",
    )
    pairs = hw // 2
    (grads,) = vmem_call(
        grads_body, [((docs * pairs, 2 * width), F32)], [mine, swap(mine), weights, weights2],
        scratch=[VMEM((2, hw, slots), F32)], name="grads",
    )
    grads = (grads + move(grads, lambda z, s: (z, s ^ 3))) + (
        move(grads, lambda z, s: (z, s ^ 5)) + move(grads, lambda z, s: (z, s ^ 6)))
    m1 = move(grads, lambda z, s: (z ^ 1, s ^ 1))
    m2 = move(grads, lambda z, s: (z ^ 2, s ^ 1))
    m3 = move(grads, lambda z, s: (z ^ 3, s))
    lanes = -(-(2 * ntest + ndocs) // 128) * 128
    (mine,) = vmem_call(
        products_body, [((ndocs, lanes), F32)],
        [grads, m1, m2, m3, t_own, t_far],
        scratch=[VMEM((ndp * docs * pairs, 2 * width), F32)], name="products",
    )
    return pl.pallas_call(
        solve_body,
        out_shape=jax.ShapeDtypeStruct((ndocs, ntest), F32),
        in_specs=[pl.BlockSpec(memory_space=VMEM)] * 3,
        out_specs=pl.BlockSpec(memory_space=VMEM),
        name="solve",
    )(*in_vmem(mine, swap(mine), rows))


def solution(mesh):
    in_specs = (
        P("dp", "seq", None),
        P("dp", "seq", None),
        P("dp", "seq"),
        P("dp", None),
        P(),
        P("seq", None),
        P("seq", None),
        P("seq", None),
    )
    fast = mesh.shape["seq"] == 8 and mesh.shape["dp"] == 4
    return jax.shard_map(
        paired_chips if fast else any_mesh,
        mesh=mesh, in_specs=in_specs, out_specs=P(None, "seq"), check_vma=False,
    )
```

```python
import functools

import jax
import jax.numpy as jnp
from jax import lax
from jax.experimental import pallas as pl
from jax.experimental.pallas import tpu as pltpu
from jax.sharding import PartitionSpec as P

BLOCK = 128
HIGH = lax.Precision.HIGHEST
F32 = jnp.float32
VMEM = pltpu.VMEM
LIMIT = 16 * 1024 * 1024


def any_mesh(inputs, out_grads, valid, doc_blocks, doc_ids, proj_in, proj_out, test_grads):
    px = jnp.dot(inputs[0], lax.all_gather(proj_in, "seq", tiled=True), preferred_element_type=F32)
    pg = jnp.dot(out_grads[0], lax.all_gather(proj_out, "seq", tiled=True), preferred_element_type=F32)
    slots = px.shape[0]
    ends = jnp.cumsum(doc_blocks[0])
    position = lax.axis_index("seq") * slots + jnp.arange(slots, dtype=jnp.int32)
    owner = jnp.sum((position // BLOCK)[:, None] >= ends[None, :], axis=1)
    mine = owner[None, :] == jnp.arange(ends.shape[0])[:, None]
    weights = (mine & (valid[0][None, :] == 1)).astype(F32)
    weighted = weights[:, None, :] * pg.T[None, :, :]
    grads = jnp.einsum("jat,tb->jab", weighted, px, precision=HIGH)
    grads = lax.psum(grads.reshape(grads.shape[0], -1), "seq")
    grads = lax.all_gather(grads, "dp", tiled=True)
    gram = jnp.dot(grads, grads.T, precision=HIGH)
    cross = jnp.dot(grads, test_grads.astype(F32).T, precision=HIGH)
    ndocs = gram.shape[0]
    damp = 0.1 * jnp.trace(gram) / ndocs
    factor = jnp.linalg.cholesky(gram / ndocs + damp * jnp.eye(ndocs, dtype=F32))
    middle = lax.linalg.triangular_solve(factor, cross, left_side=True, lower=True)
    solved = lax.linalg.triangular_solve(factor, middle, left_side=True, lower=True, transpose_a=True)
    placing = (doc_ids[None, :] == jnp.arange(ndocs, dtype=jnp.int32)[:, None]).astype(F32)
    return jnp.dot(placing, solved, precision=HIGH)


def place(seq, dp):
    bits = seq ^ (seq >> 1) ^ (seq >> 2) ^ (dp >> 1)
    return bits & 1


def here():
    seq, dp = lax.axis_index("seq"), lax.axis_index("dp")
    return seq, dp, place(seq, dp)


def in_vmem(*arrays):
    return [pltpu.with_memory_space_constraint(x, VMEM) for x in arrays]


def vmem_call(body, outs, args, hbm=(), scratch=(), name=None, moved=0):
    specs = [pl.BlockSpec(memory_space=VMEM)] * len(args) + [pl.BlockSpec(memory_space=pltpu.HBM)] * len(hbm)
    far = [pltpu.with_memory_space_constraint(x, pltpu.HBM) for x in hbm]
    return pl.pallas_call(
        body,
        out_shape=[VMEM(s, d) for s, d in outs],
        in_specs=specs,
        out_specs=[pl.BlockSpec(memory_space=VMEM)] * len(outs),
        scratch_shapes=list(scratch),
        name=name,
        compiler_params=pltpu.CompilerParams(vmem_limit_bytes=LIMIT),
        cost_estimate=pl.CostEstimate(flops=0, transcendentals=0, bytes_accessed=moved),
    )(*in_vmem(*args), *far)


def source(seq, slot):
    even, odd = ((0, 0), (5, 3), (3, 5), (6, 6))[slot]
    return seq ^ jnp.where(seq & 1 == 0, even, odd)


def weights_body(valid, blocks, out_t, in_t, first, second, whole, weights, valid_v, blocks_s, sems):
    seq, _, _ = here()
    rows_out, rows_in, size = out_t.shape[1], in_t.shape[1], first.shape[1]
    rest = rows_out - size
    copies = [
        pltpu.make_async_copy(out_t.at[:, pl.ds(0, size)], first, sems.at[0]),
        pltpu.make_async_copy(out_t.at[:, pl.ds(size, rest)], second.at[:, pl.ds(0, rest)], sems.at[1]),
        pltpu.make_async_copy(in_t, second.at[:, pl.ds(rest, rows_in)], sems.at[2]),
        pltpu.make_async_copy(out_t, whole.at[:, pl.ds(0, rows_out)], sems.at[3]),
        pltpu.make_async_copy(in_t, whole.at[:, pl.ds(rows_out, rows_in)], sems.at[4]),
        pltpu.make_async_copy(valid, valid_v, sems.at[5]),
        pltpu.make_async_copy(blocks, blocks_s, sems.at[6]),
    ]
    for c in copies:
        c.start()
    for c in copies:
        c.wait()
    slots = valid.shape[1]
    blk = (seq * slots + lax.broadcasted_iota(jnp.int32, weights.shape, 1)) // BLOCK
    row = lax.broadcasted_iota(jnp.int32, weights.shape, 0)
    owner = jnp.zeros_like(blk)
    end = 0
    for j in range(blocks.shape[1]):
        end = end + blocks_s[0, j]
        owner = owner + (blk >= end).astype(jnp.int32)
    weights[...] = jnp.where((owner == row) & (valid_v[...] == 1), 1.0, 0.0)


def column_copies(og, inp, three, last, mine, sems):
    nseq = lax.axis_size("seq")
    wo, wi = og.shape[1] // nseq, inp.shape[1] // nseq
    copies = []
    for k in range(4):
        shard = source(mine, k)
        out, base = (last, 0) if k == 3 else (three, k * (wo + wi))
        copies.append(pltpu.make_async_copy(
            og.at[:, pl.ds(pl.multiple_of(shard * wo, wo), wo)], out.at[:, pl.ds(base, wo)], sems.at[2 * k]))
        copies.append(pltpu.make_async_copy(
            inp.at[:, pl.ds(pl.multiple_of(shard * wi, wi), wi)], out.at[:, pl.ds(base + wo, wi)], sems.at[2 * k + 1]))
    return copies


def nt(a, b, precision=None):
    return lax.dot_general(a, b, (((1,), (1,)), ((), ())), precision=precision, preferred_element_type=F32)


def project(w, near, base, far, shard, width, skip):
    rows = w.shape[1]
    start = pl.multiple_of(shard * width + skip, 128)
    return nt(w, jnp.concatenate([near[:, pl.ds(base, rows)], far[:, pl.ds(start, rows)]], axis=0))


def near_body(own, a1, a2, b, og2, inp2, og, inp, tests, ids, pg, px, near, t_own, t_far, rows,
              near_s, ids_s, sems, *, wi, wo):
    seq, _, half = here()
    hf = t_own.shape[1]
    size = a1.shape[1]
    rest = wo - size
    each = wo + wi
    copies = column_copies(og, inp, near_s, near, seq, sems)
    more = [
        pltpu.make_async_copy(tests.at[:, pl.ds(pl.multiple_of(half * hf, hf), hf)], t_own, sems.at[8]),
        pltpu.make_async_copy(tests.at[:, pl.ds(pl.multiple_of((1 - half) * hf, hf), hf)], t_far, sems.at[9]),
        pltpu.make_async_copy(ids, ids_s, sems.at[10]),
    ]
    for c in copies + more:
        c.start()
    total, total_x = 0.0, 0.0
    for k, w in ((0, own), (2, b), (1, None)):
        base, shard = k * each, source(seq, k)
        copies[2 * k].wait()
        copies[2 * k + 1].wait()
        if w is None:
            total = total + project(a1[...], near_s, base, og2, shard, wo, 0)
            total = total + project(a2[:, :rest], near_s, base + size, og2, shard, wo, size)
            total_x = total_x + project(a2[:, rest:], near_s, base + wo, inp2, shard, wi, 0)
        else:
            total = total + project(w[:, :wo], near_s, base, og2, shard, wo, 0)
            total_x = total_x + project(w[:, wo:], near_s, base + wo, inp2, shard, wi, 0)
    pg[...] = total
    px[...] = total_x
    for c in copies[6:] + more:
        c.wait()
    for r in range(rows.shape[0]):
        rows[r:r + 1, :] = jnp.full((1, rows.shape[1]), ids_s[r], jnp.int32)


def diagonal_body(c1, pg_in, near, og2, pg, *, wo):
    seq, _, _ = here()
    pg[...] = pg_in[...] + project(c1[...], near, 0, og2, source(seq, 3), wo, 0)


def last_body(c2, pg_in, px_in, near, og2, inp2, out, *, wi, wo):
    seq, _, _ = here()
    rest = c2.shape[1] - wi
    rows = pg_in.shape[0]
    shard = source(seq, 3)
    out[:rows] = pg_in[...] + project(c2[:, :rest], near, wo - rest, og2, shard, wo, wo - rest)
    out[rows:2 * rows] = px_in[...] + project(c2[:, rest:], near, wo, inp2, shard, wi, 0)


def grads_body(mine, far, weights, weights2, grads, pgs):
    _, _, half = here()
    slots = pgs.shape[2]
    rows = mine.shape[0] // 2
    hw = rows // 2
    pairs = hw // 2
    docs = grads.shape[0] // pairs
    both = []
    for base in (0, rows):
        block = pl.ds(base, rows)
        both.append([mine[block, :slots] + far[block, slots:], mine[block, slots:] + far[block, :slots]])
    for u in range(2):
        pgs[u] = jnp.where(half == 1, both[0][u][hw:], both[0][u][:hw])
    px = jnp.concatenate(both[1], axis=1)
    tokens = jnp.concatenate([weights[...], weights2[...]], axis=1)
    parts = []
    for q in range(2):
        some = jnp.concatenate([pgs[u, pl.ds(q, pairs, stride=2), :] for u in range(2)], axis=1)
        weighted = jnp.concatenate([some * tokens[j:j + 1, :] for j in range(docs)], axis=0)
        parts.append(nt(weighted, px, HIGH))
    grads[...] = jnp.concatenate(parts, axis=1)


def sum_body(own, px, py, pd, out):
    out[...] = (own[...] + px[...]) + (py[...] + pd[...])


def products_body(m0, m3, m2, m1, t_own, t_far, out, every):
    seq, dp, _ = here()
    rows = m0.shape[0]
    for k, m in zip((0, 3, 2, 1), (m0, m3, m2, m1)):
        every[pl.ds(pl.multiple_of((dp ^ k) * rows, rows), rows), :] = m[...]
    docs = out.shape[0]
    pairs = every.shape[0] // docs
    flat = jnp.concatenate([every[pl.ds(i, docs, stride=pairs), :] for i in range(pairs)], axis=1)
    gram = nt(flat, flat, HIGH)
    own, far = t_own[...], t_far[...]
    core = seq & 1
    tests = jnp.concatenate([jnp.where(core == 0, own, far), jnp.where(core == 0, far, own)], axis=0)
    high = flat.astype(jnp.bfloat16)
    rest = flat - high.astype(F32)
    mid = rest.astype(jnp.bfloat16)
    low = (rest - mid.astype(F32)).astype(jnp.bfloat16)
    cross = nt(low, tests) + nt(mid, tests) + nt(high, tests)
    pad = jnp.zeros((docs, out.shape[1] - cross.shape[1] - docs), F32)
    out[...] = jnp.concatenate([cross, gram, pad], axis=1)


def solve_body(mine, far, rows, out):
    docs, tests = out.shape
    seq, _, _ = here()
    both = mine[...] + far[...]
    shape = both.shape
    row = lax.broadcasted_iota(jnp.int32, shape, 0)
    columns = [jnp.broadcast_to(both[:, 2 * tests + k:2 * tests + k + 1], shape) for k in range(docs)]
    trace = columns[0][0:1, :]
    for k in range(1, docs):
        trace = trace + columns[k][k:k + 1, :]
    damp = 0.1 * trace / docs
    columns = [c / docs + jnp.where(row == k, damp, 0.0) for k, c in enumerate(columns)]
    scale = jnp.zeros(shape, F32)
    for k in range(docs):
        inverse = 1.0 / columns[k][k:k + 1, :]
        scale = jnp.where(row == k, inverse, scale)
        factor = jnp.where(row == k, 0.0, columns[k] * inverse)
        both = both - factor * both[k:k + 1, :]
        for j in range(k + 1, docs):
            columns[j] = columns[j] - factor * columns[j][k:k + 1, :]
    solved = both * scale
    placed = jnp.zeros(shape, F32)
    for r in range(docs):
        placed = jnp.where(row == rows[r:r + 1, :], solved[r:r + 1, :], placed)
    out[...] = jnp.where(seq & 1 == 0, placed[:, :tests], placed[:, tests:2 * tests])


def paired_chips(inputs, out_grads, valid, doc_blocks, doc_ids, proj_in, proj_out, test_grads):
    ndp, nseq = lax.axis_size("dp"), lax.axis_size("seq")
    docs = doc_blocks.shape[1]
    ndocs = docs * ndp
    inp, og = inputs[0], out_grads[0]
    width = proj_out.shape[1]
    hw = width // 2
    wo, wi = proj_out.shape[0], proj_in.shape[0]
    slots = og.shape[0]
    ntest, feat = test_grads.shape
    bf = jnp.bfloat16

    def move(x, to):
        pairs = [(z * nseq + s, (lambda t: t[0] * nseq + t[1])(to(z, s))) for z in range(ndp) for s in range(nseq)]
        return lax.ppermute(x, ("dp", "seq"), pairs)

    def swap(x):
        return move(x, lambda z, s: (z, s ^ 1))

    def ring(x, step):
        return move(x, lambda z, s: (z, s ^ ((3, 5)[(s & 1) ^ step])))

    size = (wo + wi) // 256 * 128
    first, second, whole, weights = vmem_call(
        weights_body,
        [((width, size), bf), ((width, wo + wi - size), bf), ((width, wo + wi), bf), ((8, slots), F32)],
        [], hbm=[valid, doc_blocks, proj_out.T, proj_in.T],
        scratch=[VMEM((1, slots), jnp.int32), pltpu.SMEM((1, docs), jnp.int32), pltpu.SemaphoreType.DMA((7,))],
        name="weights",
    )
    a1, a2, b = ring(first, 0), ring(second, 0), ring(whole, 1)
    weights2 = swap(weights)
    og2, inp2 = swap(og), swap(inp)
    c1 = ring(a1, 0)
    c2 = ring(a2, 0)
    part = ((width, 2 * slots), F32)
    lanes = -(-(2 * ntest + ndocs) // 128) * 128
    pg, px, near, t_own, t_send, rows = vmem_call(
        functools.partial(near_body, wi=wi, wo=wo),
        [part, part, ((slots, wo + wi), bf)] + [((ntest, feat // 2), bf)] * 2 + [((ndocs, lanes), jnp.int32)],
        [whole, a1, a2, b, og2, inp2], hbm=[og, inp, test_grads, doc_ids],
        scratch=[VMEM((slots, 3 * (wo + wi)), bf), pltpu.SMEM((ndocs,), jnp.int32), pltpu.SemaphoreType.DMA((11,))],
        name="near",
    )
    t_far = swap(t_send)
    (pg,) = vmem_call(functools.partial(diagonal_body, wo=wo), [part], [c1, pg, near, og2], name="diagonal")
    (mine,) = vmem_call(
        functools.partial(last_body, wi=wi, wo=wo), [((2 * width, 2 * slots), F32)],
        [c2, pg, px, near, og2, inp2], name="last",
    )
    pairs = hw // 2
    (grads,) = vmem_call(
        grads_body, [((docs * pairs, 2 * width), F32)], [mine, swap(mine), weights, weights2],
        scratch=[VMEM((2, hw, slots), F32)], name="grads",
    )
    px = move(grads, lambda z, s: (z, s ^ 3))
    py = move(grads, lambda z, s: (z, s ^ 5))
    pd = move(grads, lambda z, s: (z, s ^ 6))
    grads = (grads + px) + (py + pd)
    m3 = move(grads, lambda z, s: (z ^ 3, s ^ 1))
    m2 = move(grads, lambda z, s: (z ^ 2, s ^ 1))
    m1 = move(grads, lambda z, s: (z ^ 1, s))
    (mine,) = vmem_call(
        products_body, [((ndocs, lanes), F32)],
        [grads, m3, m2, m1, t_own, t_far],
        scratch=[VMEM((ndp * docs * pairs, 2 * width), F32)], name="products",
    )
    return pl.pallas_call(
        solve_body,
        out_shape=jax.ShapeDtypeStruct((ndocs, ntest), F32),
        in_specs=[pl.BlockSpec(memory_space=VMEM)] * 3,
        out_specs=pl.BlockSpec(memory_space=VMEM),
        name="solve",
    )(*in_vmem(mine, swap(mine), rows))


def solution(mesh):
    in_specs = (
        P("dp", "seq", None),
        P("dp", "seq", None),
        P("dp", "seq"),
        P("dp", None),
        P(),
        P("seq", None),
        P("seq", None),
        P("seq", None),
    )
    fast = mesh.shape["seq"] == 8 and mesh.shape["dp"] == 4
    return jax.shard_map(
        paired_chips if fast else any_mesh,
        mesh=mesh, in_specs=in_specs, out_specs=P(None, "seq"), check_vma=False,
    )
```

```python
import functools

import jax
import jax.numpy as jnp
from jax import lax
from jax.experimental import pallas as pl
from jax.experimental.pallas import tpu as pltpu
from jax.sharding import PartitionSpec as P

BLOCK = 128
HIGH = lax.Precision.HIGHEST
F32 = jnp.float32
VMEM = pltpu.VMEM
LIMIT = 16 * 1024 * 1024


def any_mesh(inputs, out_grads, valid, doc_blocks, doc_ids, proj_in, proj_out, test_grads):
    px = jnp.dot(inputs[0], lax.all_gather(proj_in, "seq", tiled=True), preferred_element_type=F32)
    pg = jnp.dot(out_grads[0], lax.all_gather(proj_out, "seq", tiled=True), preferred_element_type=F32)
    slots = px.shape[0]
    ends = jnp.cumsum(doc_blocks[0])
    position = lax.axis_index("seq") * slots + jnp.arange(slots, dtype=jnp.int32)
    owner = jnp.sum((position // BLOCK)[:, None] >= ends[None, :], axis=1)
    mine = owner[None, :] == jnp.arange(ends.shape[0])[:, None]
    weights = (mine & (valid[0][None, :] == 1)).astype(F32)
    weighted = weights[:, None, :] * pg.T[None, :, :]
    grads = jnp.einsum("jat,tb->jab", weighted, px, precision=HIGH)
    grads = lax.psum(grads.reshape(grads.shape[0], -1), "seq")
    grads = lax.all_gather(grads, "dp", tiled=True)
    gram = jnp.dot(grads, grads.T, precision=HIGH)
    cross = jnp.dot(grads, test_grads.astype(F32).T, precision=HIGH)
    ndocs = gram.shape[0]
    damp = 0.1 * jnp.trace(gram) / ndocs
    factor = jnp.linalg.cholesky(gram / ndocs + damp * jnp.eye(ndocs, dtype=F32))
    middle = lax.linalg.triangular_solve(factor, cross, left_side=True, lower=True)
    solved = lax.linalg.triangular_solve(factor, middle, left_side=True, lower=True, transpose_a=True)
    placing = (doc_ids[None, :] == jnp.arange(ndocs, dtype=jnp.int32)[:, None]).astype(F32)
    return jnp.dot(placing, solved, precision=HIGH)


def place(seq, dp):
    bits = seq ^ (seq >> 1) ^ (seq >> 2) ^ (dp >> 1)
    return bits & 1


def here():
    seq, dp = lax.axis_index("seq"), lax.axis_index("dp")
    return seq, dp, place(seq, dp)


def in_vmem(*arrays):
    return [pltpu.with_memory_space_constraint(x, VMEM) for x in arrays]


def vmem_call(body, outs, args, hbm=(), scratch=(), name=None, moved=0):
    specs = [pl.BlockSpec(memory_space=VMEM)] * len(args) + [pl.BlockSpec(memory_space=pltpu.HBM)] * len(hbm)
    far = [pltpu.with_memory_space_constraint(x, pltpu.HBM) for x in hbm]
    return pl.pallas_call(
        body,
        out_shape=[VMEM(s, d) for s, d in outs],
        in_specs=specs,
        out_specs=[pl.BlockSpec(memory_space=VMEM)] * len(outs),
        scratch_shapes=list(scratch),
        name=name,
        compiler_params=pltpu.CompilerParams(vmem_limit_bytes=LIMIT),
        cost_estimate=pl.CostEstimate(flops=0, transcendentals=0, bytes_accessed=moved),
    )(*in_vmem(*args), *far)


def source(seq, slot):
    even, odd = ((0, 0), (5, 3), (3, 5), (6, 6))[slot]
    return seq ^ jnp.where(seq & 1 == 0, even, odd)


def weights_body(valid, blocks, out_t, in_t, first, second, whole, weights, valid_v, blocks_s, sems):
    seq, _, _ = here()
    rows_out, rows_in, size = out_t.shape[1], in_t.shape[1], first.shape[1]
    rest = rows_out - size
    copies = [
        pltpu.make_async_copy(out_t.at[:, pl.ds(0, size)], first, sems.at[0]),
        pltpu.make_async_copy(out_t.at[:, pl.ds(size, rest)], second.at[:, pl.ds(0, rest)], sems.at[1]),
        pltpu.make_async_copy(in_t, second.at[:, pl.ds(rest, rows_in)], sems.at[2]),
        pltpu.make_async_copy(out_t, whole.at[:, pl.ds(0, rows_out)], sems.at[3]),
        pltpu.make_async_copy(in_t, whole.at[:, pl.ds(rows_out, rows_in)], sems.at[4]),
        pltpu.make_async_copy(valid, valid_v, sems.at[5]),
        pltpu.make_async_copy(blocks, blocks_s, sems.at[6]),
    ]
    for c in copies:
        c.start()
    for c in copies:
        c.wait()
    slots = valid.shape[1]
    blk = (seq * slots + lax.broadcasted_iota(jnp.int32, weights.shape, 1)) // BLOCK
    row = lax.broadcasted_iota(jnp.int32, weights.shape, 0)
    owner = jnp.zeros_like(blk)
    end = 0
    for j in range(blocks.shape[1]):
        end = end + blocks_s[0, j]
        owner = owner + (blk >= end).astype(jnp.int32)
    weights[...] = jnp.where((owner == row) & (valid_v[...] == 1), 1.0, 0.0)


def column_copies(og, inp, three, last, mine, sems):
    nseq = lax.axis_size("seq")
    wo, wi = og.shape[1] // nseq, inp.shape[1] // nseq
    copies = []
    for k in range(4):
        shard = source(mine, k)
        out, base = (last, 0) if k == 3 else (three, k * (wo + wi))
        copies.append(pltpu.make_async_copy(
            og.at[:, pl.ds(pl.multiple_of(shard * wo, wo), wo)], out.at[:, pl.ds(base, wo)], sems.at[2 * k]))
        copies.append(pltpu.make_async_copy(
            inp.at[:, pl.ds(pl.multiple_of(shard * wi, wi), wi)], out.at[:, pl.ds(base + wo, wi)], sems.at[2 * k + 1]))
    return copies


def nt(a, b, precision=None):
    return lax.dot_general(a, b, (((1,), (1,)), ((), ())), precision=precision, preferred_element_type=F32)


def project(w, near, base, far, shard, width, skip):
    rows = w.shape[1]
    start = pl.multiple_of(shard * width + skip, 128)
    return nt(w, jnp.concatenate([near[:, pl.ds(base, rows)], far[:, pl.ds(start, rows)]], axis=0))


def keep_body(_, og, inp, tests, ids, near, late, t_own, t_far, rows, ids_s, sems):
    seq, _, half = here()
    hf = t_own.shape[1]
    copies = column_copies(og, inp, near, late, seq, sems)
    copies.append(pltpu.make_async_copy(tests.at[:, pl.ds(pl.multiple_of(half * hf, hf), hf)], t_own, sems.at[8]))
    copies.append(pltpu.make_async_copy(tests.at[:, pl.ds(pl.multiple_of((1 - half) * hf, hf), hf)], t_far, sems.at[9]))
    copies.append(pltpu.make_async_copy(ids, ids_s, sems.at[10]))
    for c in copies:
        c.start()
    for c in copies:
        c.wait()
    for r in range(rows.shape[0]):
        rows[r:r + 1, :] = jnp.full((1, rows.shape[1]), ids_s[r], jnp.int32)


def after_body(x, _, out):
    out[...] = x[...]


def near_body(own, a1, a2, b, og2, inp2, near, pg, px, *, wi, wo):
    seq, _, _ = here()
    size = a1.shape[1]
    rest = wo - size
    total, total_x = 0.0, 0.0
    for k, w in ((0, own), (2, b), (1, None)):
        base, shard = k * (wo + wi), source(seq, k)
        if w is None:
            total = total + project(a1[...], near, base, og2, shard, wo, 0)
            total = total + project(a2[:, :rest], near, base + size, og2, shard, wo, size)
            total_x = total_x + project(a2[:, rest:], near, base + wo, inp2, shard, wi, 0)
        else:
            total = total + project(w[:, :wo], near, base, og2, shard, wo, 0)
            total_x = total_x + project(w[:, wo:], near, base + wo, inp2, shard, wi, 0)
    pg[...] = total
    px[...] = total_x


def diagonal_body(c1, pg_in, near, og2, pg, *, wo):
    seq, _, _ = here()
    pg[...] = pg_in[...] + project(c1[...], near, 0, og2, source(seq, 3), wo, 0)


def last_body(c2, pg_in, px_in, near, og2, inp2, weights, out, *, wi, wo):
    seq, _, _ = here()
    rest = c2.shape[1] - wi
    rows = pg_in.shape[0]
    shard = source(seq, 3)
    out[:rows] = pg_in[...] + project(c2[:, :rest], near, wo - rest, og2, shard, wo, wo - rest)
    out[rows:2 * rows] = px_in[...] + project(c2[:, rest:], near, wo, inp2, shard, wi, 0)
    out[2 * rows:] = jnp.concatenate([weights[...], jnp.zeros_like(weights)], axis=1)


def halves(x):
    high = x.astype(jnp.bfloat16)
    return [high, (x - high.astype(F32)).astype(jnp.bfloat16)]


def grads_body(mine, far, grads, pgs):
    _, _, half = here()
    slots = pgs.shape[2]
    rows = (mine.shape[0] - 8) // 2
    hw = rows // 2
    pairs = hw // 2
    docs = grads.shape[0] // pairs
    both = []
    for base in (0, rows):
        block = pl.ds(base, rows)
        both.append([mine[block, :slots] + far[block, slots:], mine[block, slots:] + far[block, :slots]])
    for u in range(2):
        pgs[u] = jnp.where(half == 1, both[0][u][hw:], both[0][u][:hw])
    px = jnp.concatenate(both[1], axis=1)
    tokens = jnp.concatenate([mine[2 * rows:, :slots], far[2 * rows:, :slots]], axis=1)
    parts = []
    for q in range(2):
        some = jnp.concatenate([pgs[u, pl.ds(q, pairs, stride=2), :] for u in range(2)], axis=1)
        weighted = jnp.concatenate([some * tokens[j:j + 1, :] for j in range(docs)], axis=0)
        parts.append(nt(weighted, px, HIGH))
    grads[...] = jnp.concatenate(parts, axis=1)


def sum_body(own, px, py, pd, out):
    out[...] = (own[...] + px[...]) + (py[...] + pd[...])


def products_body(m0, m3, m2, m1, t_own, t_far, out, every):
    seq, dp, _ = here()
    rows = m0.shape[0]
    for k, m in zip((0, 3, 2, 1), (m0, m3, m2, m1)):
        every[pl.ds(pl.multiple_of((dp ^ k) * rows, rows), rows), :] = m[...]
    docs = out.shape[0]
    pairs = every.shape[0] // docs
    flat = jnp.concatenate([every[pl.ds(i, docs, stride=pairs), :] for i in range(pairs)], axis=1)
    own, far = t_own[...], t_far[...]
    core = seq & 1
    high, low = halves(flat)
    ntest = 2 * own.shape[0]
    right = [jnp.where(core == 0, own, far), jnp.where(core == 0, far, own), high, low]
    both = nt(jnp.concatenate([high, low], axis=0), jnp.concatenate(right, axis=0))
    top, bottom = both[:docs], both[docs:]
    cross = top[:, :ntest] + bottom[:, :ntest]
    gram = top[:, ntest:ntest + docs] + (top[:, ntest + docs:] + bottom[:, ntest:ntest + docs])
    pad = jnp.zeros((docs, out.shape[1] - cross.shape[1] - docs), F32)
    out[...] = jnp.concatenate([cross, gram, pad], axis=1)


def solve_body(mine, far, rows, out):
    docs, tests = out.shape
    seq, _, _ = here()
    both = mine[...] + far[...]
    shape = both.shape
    row = lax.broadcasted_iota(jnp.int32, shape, 0)
    columns = [jnp.broadcast_to(both[:, 2 * tests + k:2 * tests + k + 1], shape) for k in range(docs)]
    trace = columns[0][0:1, :]
    for k in range(1, docs):
        trace = trace + columns[k][k:k + 1, :]
    damp = 0.1 * trace / docs
    columns = [c / docs + jnp.where(row == k, damp, 0.0) for k, c in enumerate(columns)]
    scale = jnp.zeros(shape, F32)
    for k in range(docs):
        inverse = 1.0 / columns[k][k:k + 1, :]
        scale = jnp.where(row == k, inverse, scale)
        factor = jnp.where(row == k, 0.0, columns[k] * inverse)
        both = both - factor * both[k:k + 1, :]
        for j in range(k + 1, docs):
            columns[j] = columns[j] - factor * columns[j][k:k + 1, :]
    solved = both * scale
    placed = jnp.zeros(shape, F32)
    for r in range(docs):
        placed = jnp.where(row == rows[r:r + 1, :], solved[r:r + 1, :], placed)
    out[...] = jnp.where(seq & 1 == 0, placed[:, :tests], placed[:, tests:2 * tests])


def paired_chips(inputs, out_grads, valid, doc_blocks, doc_ids, proj_in, proj_out, test_grads):
    ndp, nseq = lax.axis_size("dp"), lax.axis_size("seq")
    docs = doc_blocks.shape[1]
    ndocs = docs * ndp
    inp, og = inputs[0], out_grads[0]
    width = proj_out.shape[1]
    hw = width // 2
    wo, wi = proj_out.shape[0], proj_in.shape[0]
    slots = og.shape[0]
    ntest, feat = test_grads.shape
    bf = jnp.bfloat16

    def move(x, to):
        pairs = [(z * nseq + s, (lambda t: t[0] * nseq + t[1])(to(z, s))) for z in range(ndp) for s in range(nseq)]
        return lax.ppermute(x, ("dp", "seq"), pairs)

    def swap(x):
        return move(x, lambda z, s: (z, s ^ 1))

    def ring(x, step):
        return move(x, lambda z, s: (z, s ^ ((3, 5)[(s & 1) ^ step])))

    size = (wo + wi) * 5 // 8 // 128 * 128
    first, second, whole, weights = vmem_call(
        weights_body,
        [((width, size), bf), ((width, wo + wi - size), bf), ((width, wo + wi), bf), ((8, slots), F32)],
        [], hbm=[valid, doc_blocks, proj_out.T, proj_in.T],
        scratch=[VMEM((1, slots), jnp.int32), pltpu.SMEM((1, docs), jnp.int32), pltpu.SemaphoreType.DMA((7,))],
        name="weights",
    )
    a1, a2, b = ring(first, 0), ring(second, 0), ring(whole, 1)
    og2, inp2 = swap(og), swap(inp)
    lanes = -(-(2 * ntest + ndocs) // 128) * 128
    three, near, t_own, t_send, rows = vmem_call(
        keep_body,
        [((slots, 3 * (wo + wi)), bf), ((slots, wo + wi), bf)] + [((ntest, feat // 2), bf)] * 2 + [((ndocs, lanes), jnp.int32)],
        [whole], hbm=[og, inp, test_grads, doc_ids],
        scratch=[pltpu.SMEM((ndocs,), jnp.int32), pltpu.SemaphoreType.DMA((11,))], name="keep",
    )
    (a1,) = vmem_call(after_body, [(a1.shape, bf)], [a1, rows], name="after")
    c1 = ring(a1, 0)
    c2 = ring(a2, 0)
    part = ((width, 2 * slots), F32)
    pg, px = vmem_call(
        functools.partial(near_body, wi=wi, wo=wo), [part, part], [whole, a1, a2, b, og2, inp2, three], name="near",
    )
    (pg,) = vmem_call(functools.partial(diagonal_body, wo=wo), [part], [c1, pg, near, og2], name="diagonal")
    (mine,) = vmem_call(
        functools.partial(last_body, wi=wi, wo=wo), [((2 * width + 8, 2 * slots), F32)],
        [c2, pg, px, near, og2, inp2, weights], name="last",
    )
    pairs = hw // 2
    (grads,) = vmem_call(
        grads_body, [((docs * pairs, 2 * width), F32)], [mine, swap(mine)],
        scratch=[VMEM((2, hw, slots), F32)], name="grads",
    )
    px = move(grads, lambda z, s: (z, s ^ 3))
    py = move(grads, lambda z, s: (z, s ^ 5))
    pd = move(grads, lambda z, s: (z, s ^ 6))
    grads = (grads + px) + (py + pd)
    m3 = move(grads, lambda z, s: (z ^ 3, s ^ 1))
    m2 = move(grads, lambda z, s: (z ^ 2, s ^ 1))
    m1 = move(grads, lambda z, s: (z ^ 1, s))
    t_far = swap(t_send)
    (mine,) = vmem_call(
        products_body, [((ndocs, lanes), F32)],
        [grads, m3, m2, m1, t_own, t_far],
        scratch=[VMEM((ndp * docs * pairs, 2 * width), F32)], name="products",
    )
    return pl.pallas_call(
        solve_body,
        out_shape=jax.ShapeDtypeStruct((ndocs, ntest), F32),
        in_specs=[pl.BlockSpec(memory_space=VMEM)] * 3,
        out_specs=pl.BlockSpec(memory_space=VMEM),
        name="solve",
    )(*in_vmem(mine, swap(mine), rows))


def solution(mesh):
    in_specs = (
        P("dp", "seq", None),
        P("dp", "seq", None),
        P("dp", "seq"),
        P("dp", None),
        P(),
        P("seq", None),
        P("seq", None),
        P("seq", None),
    )
    fast = mesh.shape["seq"] == 8 and mesh.shape["dp"] == 4
    return jax.shard_map(
        paired_chips if fast else any_mesh,
        mesh=mesh, in_specs=in_specs, out_specs=P(None, "seq"), check_vma=False,
    )
```

```python
import functools

import jax
import jax.numpy as jnp
from jax import lax
from jax.experimental import pallas as pl
from jax.experimental.pallas import tpu as pltpu
from jax.sharding import PartitionSpec as P

BLOCK = 128
HIGH = lax.Precision.HIGHEST
F32 = jnp.float32
VMEM = pltpu.VMEM
LIMIT = 16 * 1024 * 1024


def any_mesh(inputs, out_grads, valid, doc_blocks, doc_ids, proj_in, proj_out, test_grads):
    px = jnp.dot(inputs[0], lax.all_gather(proj_in, "seq", tiled=True), preferred_element_type=F32)
    pg = jnp.dot(out_grads[0], lax.all_gather(proj_out, "seq", tiled=True), preferred_element_type=F32)
    slots = px.shape[0]
    ends = jnp.cumsum(doc_blocks[0])
    position = lax.axis_index("seq") * slots + jnp.arange(slots, dtype=jnp.int32)
    owner = jnp.sum((position // BLOCK)[:, None] >= ends[None, :], axis=1)
    mine = owner[None, :] == jnp.arange(ends.shape[0])[:, None]
    weights = (mine & (valid[0][None, :] == 1)).astype(F32)
    weighted = weights[:, None, :] * pg.T[None, :, :]
    grads = jnp.einsum("jat,tb->jab", weighted, px, precision=HIGH)
    grads = lax.psum(grads.reshape(grads.shape[0], -1), "seq")
    grads = lax.all_gather(grads, "dp", tiled=True)
    gram = jnp.dot(grads, grads.T, precision=HIGH)
    cross = jnp.dot(grads, test_grads.astype(F32).T, precision=HIGH)
    ndocs = gram.shape[0]
    damp = 0.1 * jnp.trace(gram) / ndocs
    factor = jnp.linalg.cholesky(gram / ndocs + damp * jnp.eye(ndocs, dtype=F32))
    middle = lax.linalg.triangular_solve(factor, cross, left_side=True, lower=True)
    solved = lax.linalg.triangular_solve(factor, middle, left_side=True, lower=True, transpose_a=True)
    placing = (doc_ids[None, :] == jnp.arange(ndocs, dtype=jnp.int32)[:, None]).astype(F32)
    return jnp.dot(placing, solved, precision=HIGH)


def place(seq, dp):
    bits = seq ^ (seq >> 1) ^ (seq >> 2) ^ (dp >> 1)
    return bits & 1


def here():
    seq, dp = lax.axis_index("seq"), lax.axis_index("dp")
    return seq, dp, place(seq, dp)


def in_vmem(*arrays):
    return [pltpu.with_memory_space_constraint(x, VMEM) for x in arrays]


def vmem_call(body, outs, args, hbm=(), scratch=(), name=None, moved=0):
    specs = [pl.BlockSpec(memory_space=VMEM)] * len(args) + [pl.BlockSpec(memory_space=pltpu.HBM)] * len(hbm)
    far = [pltpu.with_memory_space_constraint(x, pltpu.HBM) for x in hbm]
    return pl.pallas_call(
        body,
        out_shape=[VMEM(s, d) for s, d in outs],
        in_specs=specs,
        out_specs=[pl.BlockSpec(memory_space=VMEM)] * len(outs),
        scratch_shapes=list(scratch),
        name=name,
        compiler_params=pltpu.CompilerParams(vmem_limit_bytes=LIMIT),
        cost_estimate=pl.CostEstimate(flops=0, transcendentals=0, bytes_accessed=moved),
    )(*in_vmem(*args), *far)


def source(seq, slot):
    even, odd = ((0, 0), (5, 3), (3, 5), (6, 6))[slot]
    return seq ^ jnp.where(seq & 1 == 0, even, odd)


def weights_body(valid, blocks, out_t, in_t, first, second, whole, weights, valid_v, blocks_s, sems):
    seq, _, _ = here()
    rows_out, rows_in, size = out_t.shape[1], in_t.shape[1], first.shape[1]
    copies = [
        pltpu.make_async_copy(valid, valid_v, sems.at[0]),
        pltpu.make_async_copy(blocks, blocks_s, sems.at[1]),
        pltpu.make_async_copy(out_t, whole.at[:, pl.ds(0, rows_out)], sems.at[2]),
        pltpu.make_async_copy(in_t, whole.at[:, pl.ds(rows_out, rows_in)], sems.at[3]),
    ]
    for c in copies:
        c.start()
    for c in copies:
        c.wait()
    first[...] = whole[:, :size]
    second[...] = whole[:, size:]
    slots = valid.shape[1]
    blk = (seq * slots + lax.broadcasted_iota(jnp.int32, weights.shape, 1)) // BLOCK
    row = lax.broadcasted_iota(jnp.int32, weights.shape, 0)
    owner = jnp.zeros_like(blk)
    end = 0
    for j in range(blocks.shape[1]):
        end = end + blocks_s[0, j]
        owner = owner + (blk >= end).astype(jnp.int32)
    weights[...] = jnp.where((owner == row) & (valid_v[...] == 1), 1.0, 0.0)


def column_copies(og, inp, three, last, mine, sems):
    nseq = lax.axis_size("seq")
    wo, wi = og.shape[1] // nseq, inp.shape[1] // nseq
    copies = []
    for k in range(4):
        shard = source(mine, k)
        out, base = (last, 0) if k == 3 else (three, k * (wo + wi))
        copies.append(pltpu.make_async_copy(
            og.at[:, pl.ds(pl.multiple_of(shard * wo, wo), wo)], out.at[:, pl.ds(base, wo)], sems.at[2 * k]))
        copies.append(pltpu.make_async_copy(
            inp.at[:, pl.ds(pl.multiple_of(shard * wi, wi), wi)], out.at[:, pl.ds(base + wo, wi)], sems.at[2 * k + 1]))
    return copies


def nt(a, b, precision=None):
    return lax.dot_general(a, b, (((1,), (1,)), ((), ())), precision=precision, preferred_element_type=F32)


def project(w, near, base, far, shard, width, skip):
    rows = w.shape[1]
    start = pl.multiple_of(shard * width + skip, 128)
    return nt(w, jnp.concatenate([near[:, pl.ds(base, rows)], far[:, pl.ds(start, rows)]], axis=0))


def keep_body(_, og, inp, tests, ids, near, late, t_own, t_far, rows, ids_s, sems):
    seq, _, half = here()
    hf = t_own.shape[1]
    copies = column_copies(og, inp, near, late, seq, sems)
    copies.append(pltpu.make_async_copy(tests.at[:, pl.ds(pl.multiple_of(half * hf, hf), hf)], t_own, sems.at[8]))
    copies.append(pltpu.make_async_copy(tests.at[:, pl.ds(pl.multiple_of((1 - half) * hf, hf), hf)], t_far, sems.at[9]))
    copies.append(pltpu.make_async_copy(ids, ids_s, sems.at[10]))
    for c in copies:
        c.start()
    for c in copies:
        c.wait()
    for r in range(rows.shape[0]):
        rows[r:r + 1, :] = jnp.full((1, rows.shape[1]), ids_s[r], jnp.int32)


def after_body(x, _, out):
    out[...] = x[...]


def near_body(own, a1, a2, b, og2, inp2, near, pg, px, *, wi, wo):
    seq, _, _ = here()
    size = a1.shape[1]
    rest = wo - size
    total, total_x = 0.0, 0.0
    for k, w in ((0, own), (2, b), (1, None)):
        base, shard = k * (wo + wi), source(seq, k)
        if w is None:
            total = total + project(a1[...], near, base, og2, shard, wo, 0)
            total = total + project(a2[:, :rest], near, base + size, og2, shard, wo, size)
            total_x = total_x + project(a2[:, rest:], near, base + wo, inp2, shard, wi, 0)
        else:
            total = total + project(w[:, :wo], near, base, og2, shard, wo, 0)
            total_x = total_x + project(w[:, wo:], near, base + wo, inp2, shard, wi, 0)
    pg[...] = total
    px[...] = total_x


def diagonal_body(c1, pg_in, near, og2, pg, *, wo):
    seq, _, _ = here()
    pg[...] = pg_in[...] + project(c1[...], near, 0, og2, source(seq, 3), wo, 0)


def last_body(c2, pg_in, px_in, near, og2, inp2, weights, out, *, wi, wo):
    seq, _, _ = here()
    rest = c2.shape[1] - wi
    rows = pg_in.shape[0]
    shard = source(seq, 3)
    out[:rows] = pg_in[...] + project(c2[:, :rest], near, wo - rest, og2, shard, wo, wo - rest)
    out[rows:2 * rows] = px_in[...] + project(c2[:, rest:], near, wo, inp2, shard, wi, 0)
    out[2 * rows:] = jnp.concatenate([weights[...], jnp.zeros_like(weights)], axis=1)


def halves(x):
    high = x.astype(jnp.bfloat16)
    return [high, (x - high.astype(F32)).astype(jnp.bfloat16)]


def grads_body(mine, far, grads, pgs):
    _, _, half = here()
    slots = pgs.shape[2]
    rows = (mine.shape[0] - 8) // 2
    hw = rows // 2
    pairs = hw // 2
    docs = grads.shape[0] // pairs
    both = []
    for base in (0, rows):
        block = pl.ds(base, rows)
        both.append([mine[block, :slots] + far[block, slots:], mine[block, slots:] + far[block, :slots]])
    for u in range(2):
        pgs[u] = jnp.where(half == 1, both[0][u][hw:], both[0][u][:hw])
    px = jnp.concatenate(both[1], axis=1)
    tokens = jnp.concatenate([mine[2 * rows:, :slots], far[2 * rows:, :slots]], axis=1)
    parts = []
    for q in range(2):
        some = jnp.concatenate([pgs[u, pl.ds(q, pairs, stride=2), :] for u in range(2)], axis=1)
        weighted = jnp.concatenate([some * tokens[j:j + 1, :] for j in range(docs)], axis=0)
        parts.append(nt(weighted, px, HIGH))
    grads[...] = jnp.concatenate(parts, axis=1)


def sum_body(own, px, py, pd, out):
    out[...] = (own[...] + px[...]) + (py[...] + pd[...])


def products_body(m0, m3, m2, m1, t_own, t_far, out, every):
    seq, dp, _ = here()
    rows = m0.shape[0]
    for k, m in zip((0, 3, 2, 1), (m0, m3, m2, m1)):
        every[pl.ds(pl.multiple_of((dp ^ k) * rows, rows), rows), :] = m[...]
    docs = out.shape[0]
    pairs = every.shape[0] // docs
    flat = jnp.concatenate([every[pl.ds(i, docs, stride=pairs), :] for i in range(pairs)], axis=1)
    own, far = t_own[...], t_far[...]
    core = seq & 1
    high, low = halves(flat)
    ntest = 2 * own.shape[0]
    right = [jnp.where(core == 0, own, far), jnp.where(core == 0, far, own), high, low]
    both = nt(jnp.concatenate([high, low], axis=0), jnp.concatenate(right, axis=0))
    top, bottom = both[:docs], both[docs:]
    cross = top[:, :ntest] + bottom[:, :ntest]
    gram = top[:, ntest:ntest + docs] + (top[:, ntest + docs:] + bottom[:, ntest:ntest + docs])
    pad = jnp.zeros((docs, out.shape[1] - cross.shape[1] - docs), F32)
    out[...] = jnp.concatenate([cross, gram, pad], axis=1)


def solve_body(mine, far, rows, out):
    docs, tests = out.shape
    seq, _, _ = here()
    both = mine[...] + far[...]
    shape = both.shape
    row = lax.broadcasted_iota(jnp.int32, shape, 0)
    columns = [jnp.broadcast_to(both[:, 2 * tests + k:2 * tests + k + 1], shape) for k in range(docs)]
    trace = columns[0][0:1, :]
    for k in range(1, docs):
        trace = trace + columns[k][k:k + 1, :]
    damp = 0.1 * trace / docs
    columns = [c / docs + jnp.where(row == k, damp, 0.0) for k, c in enumerate(columns)]
    scale = jnp.zeros(shape, F32)
    for k in range(docs):
        inverse = 1.0 / columns[k][k:k + 1, :]
        scale = jnp.where(row == k, inverse, scale)
        factor = jnp.where(row == k, 0.0, columns[k] * inverse)
        both = both - factor * both[k:k + 1, :]
        for j in range(k + 1, docs):
            columns[j] = columns[j] - factor * columns[j][k:k + 1, :]
    solved = both * scale
    placed = jnp.zeros(shape, F32)
    for r in range(docs):
        placed = jnp.where(row == rows[r:r + 1, :], solved[r:r + 1, :], placed)
    out[...] = jnp.where(seq & 1 == 0, placed[:, :tests], placed[:, tests:2 * tests])


def paired_chips(inputs, out_grads, valid, doc_blocks, doc_ids, proj_in, proj_out, test_grads):
    ndp, nseq = lax.axis_size("dp"), lax.axis_size("seq")
    docs = doc_blocks.shape[1]
    ndocs = docs * ndp
    inp, og = inputs[0], out_grads[0]
    width = proj_out.shape[1]
    hw = width // 2
    wo, wi = proj_out.shape[0], proj_in.shape[0]
    slots = og.shape[0]
    ntest, feat = test_grads.shape
    bf = jnp.bfloat16

    def move(x, to):
        pairs = [(z * nseq + s, (lambda t: t[0] * nseq + t[1])(to(z, s))) for z in range(ndp) for s in range(nseq)]
        return lax.ppermute(x, ("dp", "seq"), pairs)

    def swap(x):
        return move(x, lambda z, s: (z, s ^ 1))

    def ring(x, step):
        return move(x, lambda z, s: (z, s ^ ((3, 5)[(s & 1) ^ step])))

    size = (wo + wi) * 5 // 8 // 128 * 128
    first, second, whole, weights = vmem_call(
        weights_body,
        [((width, size), bf), ((width, wo + wi - size), bf), ((width, wo + wi), bf), ((8, slots), F32)],
        [], hbm=[valid, doc_blocks, proj_out.T, proj_in.T],
        scratch=[VMEM((1, slots), jnp.int32), pltpu.SMEM((1, docs), jnp.int32), pltpu.SemaphoreType.DMA((4,))],
        name="weights",
    )
    a1, a2, b = ring(first, 0), ring(second, 0), ring(whole, 1)
    og2, inp2 = swap(og), swap(inp)
    lanes = -(-(2 * ntest + ndocs) // 128) * 128
    three, near, t_own, t_send, rows = vmem_call(
        keep_body,
        [((slots, 3 * (wo + wi)), bf), ((slots, wo + wi), bf)] + [((ntest, feat // 2), bf)] * 2 + [((ndocs, lanes), jnp.int32)],
        [whole], hbm=[og, inp, test_grads, doc_ids],
        scratch=[pltpu.SMEM((ndocs,), jnp.int32), pltpu.SemaphoreType.DMA((11,))], name="keep",
    )
    (a1,) = vmem_call(after_body, [(a1.shape, bf)], [a1, rows], name="after")
    c1 = ring(a1, 0)
    c2 = ring(a2, 0)
    part = ((width, 2 * slots), F32)
    pg, px = vmem_call(
        functools.partial(near_body, wi=wi, wo=wo), [part, part], [whole, a1, a2, b, og2, inp2, three], name="near",
    )
    (pg,) = vmem_call(functools.partial(diagonal_body, wo=wo), [part], [c1, pg, near, og2], name="diagonal")
    (mine,) = vmem_call(
        functools.partial(last_body, wi=wi, wo=wo), [((2 * width + 8, 2 * slots), F32)],
        [c2, pg, px, near, og2, inp2, weights], name="last",
    )
    pairs = hw // 2
    (grads,) = vmem_call(
        grads_body, [((docs * pairs, 2 * width), F32)], [mine, swap(mine)],
        scratch=[VMEM((2, hw, slots), F32)], name="grads",
    )
    px = move(grads, lambda z, s: (z, s ^ 3))
    py = move(grads, lambda z, s: (z, s ^ 5))
    pd = move(grads, lambda z, s: (z, s ^ 6))
    grads = (grads + px) + (py + pd)
    m3 = move(grads, lambda z, s: (z ^ 3, s ^ 1))
    m2 = move(grads, lambda z, s: (z ^ 2, s ^ 1))
    m1 = move(grads, lambda z, s: (z ^ 1, s))
    t_far = swap(t_send)
    (mine,) = vmem_call(
        products_body, [((ndocs, lanes), F32)],
        [grads, m3, m2, m1, t_own, t_far],
        scratch=[VMEM((ndp * docs * pairs, 2 * width), F32)], name="products",
    )
    return pl.pallas_call(
        solve_body,
        out_shape=jax.ShapeDtypeStruct((ndocs, ntest), F32),
        in_specs=[pl.BlockSpec(memory_space=VMEM)] * 3,
        out_specs=pl.BlockSpec(memory_space=VMEM),
        name="solve",
    )(*in_vmem(mine, swap(mine), rows))


def solution(mesh):
    in_specs = (
        P("dp", "seq", None),
        P("dp", "seq", None),
        P("dp", "seq"),
        P("dp", None),
        P(),
        P("seq", None),
        P("seq", None),
        P("seq", None),
    )
    fast = mesh.shape["seq"] == 8 and mesh.shape["dp"] == 4
    return jax.shard_map(
        paired_chips if fast else any_mesh,
        mesh=mesh, in_specs=in_specs, out_specs=P(None, "seq"), check_vma=False,
    )
```

```python
import functools

import jax
import jax.numpy as jnp
from jax import lax
from jax.experimental import pallas as pl
from jax.experimental.pallas import tpu as pltpu
from jax.sharding import PartitionSpec as P

BLOCK = 128
HIGH = lax.Precision.HIGHEST
F32 = jnp.float32
VMEM = pltpu.VMEM
LIMIT = 16 * 1024 * 1024


def any_mesh(inputs, out_grads, valid, doc_blocks, doc_ids, proj_in, proj_out, test_grads):
    px = jnp.dot(inputs[0], lax.all_gather(proj_in, "seq", tiled=True), preferred_element_type=F32)
    pg = jnp.dot(out_grads[0], lax.all_gather(proj_out, "seq", tiled=True), preferred_element_type=F32)
    slots = px.shape[0]
    ends = jnp.cumsum(doc_blocks[0])
    position = lax.axis_index("seq") * slots + jnp.arange(slots, dtype=jnp.int32)
    owner = jnp.sum((position // BLOCK)[:, None] >= ends[None, :], axis=1)
    mine = owner[None, :] == jnp.arange(ends.shape[0])[:, None]
    weights = (mine & (valid[0][None, :] == 1)).astype(F32)
    weighted = weights[:, None, :] * pg.T[None, :, :]
    grads = jnp.einsum("jat,tb->jab", weighted, px, precision=HIGH)
    grads = lax.psum(grads.reshape(grads.shape[0], -1), "seq")
    grads = lax.all_gather(grads, "dp", tiled=True)
    gram = jnp.dot(grads, grads.T, precision=HIGH)
    cross = jnp.dot(grads, test_grads.astype(F32).T, precision=HIGH)
    ndocs = gram.shape[0]
    damp = 0.1 * jnp.trace(gram) / ndocs
    factor = jnp.linalg.cholesky(gram / ndocs + damp * jnp.eye(ndocs, dtype=F32))
    middle = lax.linalg.triangular_solve(factor, cross, left_side=True, lower=True)
    solved = lax.linalg.triangular_solve(factor, middle, left_side=True, lower=True, transpose_a=True)
    placing = (doc_ids[None, :] == jnp.arange(ndocs, dtype=jnp.int32)[:, None]).astype(F32)
    return jnp.dot(placing, solved, precision=HIGH)


def place(seq, dp):
    bits = seq ^ (seq >> 1) ^ (seq >> 2) ^ (dp >> 1)
    return bits & 1


def here():
    seq, dp = lax.axis_index("seq"), lax.axis_index("dp")
    return seq, dp, place(seq, dp)


def in_vmem(*arrays):
    return [pltpu.with_memory_space_constraint(x, VMEM) for x in arrays]


def vmem_call(body, outs, args, hbm=(), scratch=(), name=None, moved=0):
    specs = [pl.BlockSpec(memory_space=VMEM)] * len(args) + [pl.BlockSpec(memory_space=pltpu.HBM)] * len(hbm)
    far = [pltpu.with_memory_space_constraint(x, pltpu.HBM) for x in hbm]
    return pl.pallas_call(
        body,
        out_shape=[VMEM(s, d) for s, d in outs],
        in_specs=specs,
        out_specs=[pl.BlockSpec(memory_space=VMEM)] * len(outs),
        scratch_shapes=list(scratch),
        name=name,
        compiler_params=pltpu.CompilerParams(vmem_limit_bytes=LIMIT),
        cost_estimate=pl.CostEstimate(flops=0, transcendentals=0, bytes_accessed=moved),
    )(*in_vmem(*args), *far)


def source(seq, slot):
    even, odd = ((0, 0), (5, 3), (3, 5), (6, 6))[slot]
    return seq ^ jnp.where(seq & 1 == 0, even, odd)


def weights_body(valid, blocks, out_t, in_t, first, second, whole, weights, valid_v, blocks_s, sems):
    seq, _, _ = here()
    rows_out, rows_in, size = out_t.shape[1], in_t.shape[1], first.shape[1]
    copies = [
        pltpu.make_async_copy(valid, valid_v, sems.at[0]),
        pltpu.make_async_copy(blocks, blocks_s, sems.at[1]),
        pltpu.make_async_copy(out_t, whole.at[:, pl.ds(0, rows_out)], sems.at[2]),
        pltpu.make_async_copy(in_t, whole.at[:, pl.ds(rows_out, rows_in)], sems.at[3]),
    ]
    for c in copies:
        c.start()
    for c in copies:
        c.wait()
    first[...] = whole[:, :size]
    second[...] = whole[:, size:]
    slots = valid.shape[1]
    blk = (seq * slots + lax.broadcasted_iota(jnp.int32, weights.shape, 1)) // BLOCK
    row = lax.broadcasted_iota(jnp.int32, weights.shape, 0)
    owner = jnp.zeros_like(blk)
    end = 0
    for j in range(blocks.shape[1]):
        end = end + blocks_s[0, j]
        owner = owner + (blk >= end).astype(jnp.int32)
    weights[...] = jnp.where((owner == row) & (valid_v[...] == 1), 1.0, 0.0)


def column_copies(og, inp, three, last, mine, sems):
    nseq = lax.axis_size("seq")
    wo, wi = og.shape[1] // nseq, inp.shape[1] // nseq
    copies = []
    for k in range(4):
        shard = source(mine, k)
        out, base = (last, 0) if k == 3 else (three, k * (wo + wi))
        copies.append(pltpu.make_async_copy(
            og.at[:, pl.ds(pl.multiple_of(shard * wo, wo), wo)], out.at[:, pl.ds(base, wo)], sems.at[2 * k]))
        copies.append(pltpu.make_async_copy(
            inp.at[:, pl.ds(pl.multiple_of(shard * wi, wi), wi)], out.at[:, pl.ds(base + wo, wi)], sems.at[2 * k + 1]))
    return copies


def nt(a, b, precision=None):
    return lax.dot_general(a, b, (((1,), (1,)), ((), ())), precision=precision, preferred_element_type=F32)


def project(w, near, base, far, shard, width, skip):
    rows = w.shape[1]
    start = pl.multiple_of(shard * width + skip, 128)
    return nt(w, jnp.concatenate([near[:, pl.ds(base, rows)], far[:, pl.ds(start, rows)]], axis=0))


def keep_body(_, og, inp, tests, ids, near, late, t_own, t_far, rows, ids_s, sems):
    seq, _, half = here()
    hf = t_own.shape[1]
    copies = column_copies(og, inp, near, late, seq, sems)
    copies.append(pltpu.make_async_copy(tests.at[:, pl.ds(pl.multiple_of(half * hf, hf), hf)], t_own, sems.at[8]))
    copies.append(pltpu.make_async_copy(tests.at[:, pl.ds(pl.multiple_of((1 - half) * hf, hf), hf)], t_far, sems.at[9]))
    copies.append(pltpu.make_async_copy(ids, ids_s, sems.at[10]))
    for c in copies:
        c.start()
    for c in copies:
        c.wait()
    for r in range(rows.shape[0]):
        rows[r:r + 1, :] = jnp.full((1, rows.shape[1]), ids_s[r], jnp.int32)


def after_body(x, _, out):
    out[...] = x[...]


def near_body(own, a1, a2, b, og2, inp2, near, pg, px, *, wi, wo):
    seq, _, _ = here()
    size = a1.shape[1]
    rest = wo - size
    total, total_x = 0.0, 0.0
    for k, w in ((0, own), (2, b), (1, None)):
        base, shard = k * (wo + wi), source(seq, k)
        if w is None:
            total = total + project(a1[...], near, base, og2, shard, wo, 0)
            total = total + project(a2[:, :rest], near, base + size, og2, shard, wo, size)
            total_x = total_x + project(a2[:, rest:], near, base + wo, inp2, shard, wi, 0)
        else:
            total = total + project(w[:, :wo], near, base, og2, shard, wo, 0)
            total_x = total_x + project(w[:, wo:], near, base + wo, inp2, shard, wi, 0)
    pg[...] = total
    px[...] = total_x


def diagonal_body(c1, pg_in, near, og2, pg, *, wo):
    seq, _, _ = here()
    pg[...] = pg_in[...] + project(c1[...], near, 0, og2, source(seq, 3), wo, 0)


def last_body(c2, pg_in, px_in, near, og2, inp2, weights, out, *, wi, wo):
    seq, _, _ = here()
    rest = c2.shape[1] - wi
    rows = pg_in.shape[0]
    shard = source(seq, 3)
    out[:rows] = pg_in[...] + project(c2[:, :rest], near, wo - rest, og2, shard, wo, wo - rest)
    out[rows:2 * rows] = px_in[...] + project(c2[:, rest:], near, wo, inp2, shard, wi, 0)
    out[2 * rows:] = jnp.concatenate([weights[...], jnp.zeros_like(weights)], axis=1)


def halves(x):
    high = x.astype(jnp.bfloat16)
    return [high, (x - high.astype(F32)).astype(jnp.bfloat16)]


def grads_body(mine, far, grads, pgs):
    _, _, half = here()
    slots = pgs.shape[2]
    rows = (mine.shape[0] - 8) // 2
    hw = rows // 2
    pairs = hw // 2
    docs = grads.shape[0] // pairs
    both = []
    for base in (0, rows):
        block = pl.ds(base, rows)
        both.append([mine[block, :slots] + far[block, slots:], mine[block, slots:] + far[block, :slots]])
    for u in range(2):
        pgs[u] = jnp.where(half == 1, both[0][u][hw:], both[0][u][:hw])
    px = jnp.concatenate(both[1], axis=1)
    tokens = jnp.concatenate([mine[2 * rows:, :slots], far[2 * rows:, :slots]], axis=1)
    parts = []
    for q in range(2):
        some = jnp.concatenate([pgs[u, pl.ds(q, pairs, stride=2), :] for u in range(2)], axis=1)
        weighted = jnp.concatenate([some * tokens[j:j + 1, :] for j in range(docs)], axis=0)
        high, low = halves(weighted)
        px_high, px_low = halves(px)
        parts.append(nt(high, px_high) + (nt(high, px_low) + nt(low, px_high)))
    grads[...] = jnp.concatenate(parts, axis=1)


def sum_body(own, px, py, pd, out):
    out[...] = (own[...] + px[...]) + (py[...] + pd[...])


def products_body(m0, m3, m2, m1, t_own, t_far, out, every):
    seq, dp, _ = here()
    rows = m0.shape[0]
    for k, m in zip((0, 3, 2, 1), (m0, m3, m2, m1)):
        every[pl.ds(pl.multiple_of((dp ^ k) * rows, rows), rows), :] = m[...]
    docs = out.shape[0]
    pairs = every.shape[0] // docs
    flat = jnp.concatenate([every[pl.ds(i, docs, stride=pairs), :] for i in range(pairs)], axis=1)
    own, far = t_own[...], t_far[...]
    core = seq & 1
    high, low = halves(flat)
    ntest = 2 * own.shape[0]
    right = [jnp.where(core == 0, own, far), jnp.where(core == 0, far, own), high, low]
    both = nt(jnp.concatenate([high, low], axis=0), jnp.concatenate(right, axis=0))
    top, bottom = both[:docs], both[docs:]
    cross = top[:, :ntest] + bottom[:, :ntest]
    gram = top[:, ntest:ntest + docs] + (top[:, ntest + docs:] + bottom[:, ntest:ntest + docs])
    pad = jnp.zeros((docs, out.shape[1] - cross.shape[1] - docs), F32)
    out[...] = jnp.concatenate([cross, gram, pad], axis=1)


def solve_body(mine, far, rows, out):
    docs, tests = out.shape
    seq, _, _ = here()
    both = mine[...] + far[...]
    shape = both.shape
    row = lax.broadcasted_iota(jnp.int32, shape, 0)
    columns = [jnp.broadcast_to(both[:, 2 * tests + k:2 * tests + k + 1], shape) for k in range(docs)]
    trace = columns[0][0:1, :]
    for k in range(1, docs):
        trace = trace + columns[k][k:k + 1, :]
    damp = 0.1 * trace / docs
    columns = [c / docs + jnp.where(row == k, damp, 0.0) for k, c in enumerate(columns)]
    scale = jnp.zeros(shape, F32)
    for k in range(docs):
        inverse = 1.0 / columns[k][k:k + 1, :]
        scale = jnp.where(row == k, inverse, scale)
        factor = jnp.where(row == k, 0.0, columns[k] * inverse)
        both = both - factor * both[k:k + 1, :]
        for j in range(k + 1, docs):
            columns[j] = columns[j] - factor * columns[j][k:k + 1, :]
    solved = both * scale
    placed = jnp.zeros(shape, F32)
    for r in range(docs):
        placed = jnp.where(row == rows[r:r + 1, :], solved[r:r + 1, :], placed)
    out[...] = jnp.where(seq & 1 == 0, placed[:, :tests], placed[:, tests:2 * tests])


def paired_chips(inputs, out_grads, valid, doc_blocks, doc_ids, proj_in, proj_out, test_grads):
    ndp, nseq = lax.axis_size("dp"), lax.axis_size("seq")
    docs = doc_blocks.shape[1]
    ndocs = docs * ndp
    inp, og = inputs[0], out_grads[0]
    width = proj_out.shape[1]
    hw = width // 2
    wo, wi = proj_out.shape[0], proj_in.shape[0]
    slots = og.shape[0]
    ntest, feat = test_grads.shape
    bf = jnp.bfloat16

    def move(x, to):
        pairs = [(z * nseq + s, (lambda t: t[0] * nseq + t[1])(to(z, s))) for z in range(ndp) for s in range(nseq)]
        return lax.ppermute(x, ("dp", "seq"), pairs)

    def swap(x):
        return move(x, lambda z, s: (z, s ^ 1))

    def ring(x, step):
        return move(x, lambda z, s: (z, s ^ ((3, 5)[(s & 1) ^ step])))

    size = (wo + wi) * 5 // 8 // 128 * 128
    first, second, whole, weights = vmem_call(
        weights_body,
        [((width, size), bf), ((width, wo + wi - size), bf), ((width, wo + wi), bf), ((8, slots), F32)],
        [], hbm=[valid, doc_blocks, proj_out.T, proj_in.T],
        scratch=[VMEM((1, slots), jnp.int32), pltpu.SMEM((1, docs), jnp.int32), pltpu.SemaphoreType.DMA((4,))],
        name="weights",
    )
    a1, a2, b = ring(first, 0), ring(second, 0), ring(whole, 1)
    og2, inp2 = swap(og), swap(inp)
    lanes = -(-(2 * ntest + ndocs) // 128) * 128
    three, near, t_own, t_send, rows = vmem_call(
        keep_body,
        [((slots, 3 * (wo + wi)), bf), ((slots, wo + wi), bf)] + [((ntest, feat // 2), bf)] * 2 + [((ndocs, lanes), jnp.int32)],
        [whole], hbm=[og, inp, test_grads, doc_ids],
        scratch=[pltpu.SMEM((ndocs,), jnp.int32), pltpu.SemaphoreType.DMA((11,))], name="keep",
    )
    (a1,) = vmem_call(after_body, [(a1.shape, bf)], [a1, rows], name="after")
    c1 = ring(a1, 0)
    c2 = ring(a2, 0)
    part = ((width, 2 * slots), F32)
    pg, px = vmem_call(
        functools.partial(near_body, wi=wi, wo=wo), [part, part], [whole, a1, a2, b, og2, inp2, three], name="near",
    )
    (pg,) = vmem_call(functools.partial(diagonal_body, wo=wo), [part], [c1, pg, near, og2], name="diagonal")
    (mine,) = vmem_call(
        functools.partial(last_body, wi=wi, wo=wo), [((2 * width + 8, 2 * slots), F32)],
        [c2, pg, px, near, og2, inp2, weights], name="last",
    )
    pairs = hw // 2
    (grads,) = vmem_call(
        grads_body, [((docs * pairs, 2 * width), F32)], [mine, swap(mine)],
        scratch=[VMEM((2, hw, slots), F32)], name="grads",
    )
    px = move(grads, lambda z, s: (z, s ^ 3))
    py = move(grads, lambda z, s: (z, s ^ 5))
    pd = move(grads, lambda z, s: (z, s ^ 6))
    grads = (grads + px) + (py + pd)
    m3 = move(grads, lambda z, s: (z ^ 3, s ^ 1))
    m2 = move(grads, lambda z, s: (z ^ 2, s ^ 1))
    m1 = move(grads, lambda z, s: (z ^ 1, s))
    t_far = swap(t_send)
    (mine,) = vmem_call(
        products_body, [((ndocs, lanes), F32)],
        [grads, m3, m2, m1, t_own, t_far],
        scratch=[VMEM((ndp * docs * pairs, 2 * width), F32)], name="products",
    )
    return pl.pallas_call(
        solve_body,
        out_shape=jax.ShapeDtypeStruct((ndocs, ntest), F32),
        in_specs=[pl.BlockSpec(memory_space=VMEM)] * 3,
        out_specs=pl.BlockSpec(memory_space=VMEM),
        name="solve",
    )(*in_vmem(mine, swap(mine), rows))


def solution(mesh):
    in_specs = (
        P("dp", "seq", None),
        P("dp", "seq", None),
        P("dp", "seq"),
        P("dp", None),
        P(),
        P("seq", None),
        P("seq", None),
        P("seq", None),
    )
    fast = mesh.shape["seq"] == 8 and mesh.shape["dp"] == 4
    return jax.shard_map(
        paired_chips if fast else any_mesh,
        mesh=mesh, in_specs=in_specs, out_specs=P(None, "seq"), check_vma=False,
    )
```

```python
import functools

import jax
import jax.numpy as jnp
from jax import lax
from jax.experimental import pallas as pl
from jax.experimental.pallas import tpu as pltpu
from jax.sharding import PartitionSpec as P

BLOCK = 128
HIGH = lax.Precision.HIGHEST
F32 = jnp.float32
VMEM = pltpu.VMEM
LIMIT = 16 * 1024 * 1024


def any_mesh(inputs, out_grads, valid, doc_blocks, doc_ids, proj_in, proj_out, test_grads):
    px = jnp.dot(inputs[0], lax.all_gather(proj_in, "seq", tiled=True), preferred_element_type=F32)
    pg = jnp.dot(out_grads[0], lax.all_gather(proj_out, "seq", tiled=True), preferred_element_type=F32)
    slots = px.shape[0]
    ends = jnp.cumsum(doc_blocks[0])
    position = lax.axis_index("seq") * slots + jnp.arange(slots, dtype=jnp.int32)
    owner = jnp.sum((position // BLOCK)[:, None] >= ends[None, :], axis=1)
    mine = owner[None, :] == jnp.arange(ends.shape[0])[:, None]
    weights = (mine & (valid[0][None, :] == 1)).astype(F32)
    weighted = weights[:, None, :] * pg.T[None, :, :]
    grads = jnp.einsum("jat,tb->jab", weighted, px, precision=HIGH)
    grads = lax.psum(grads.reshape(grads.shape[0], -1), "seq")
    grads = lax.all_gather(grads, "dp", tiled=True)
    gram = jnp.dot(grads, grads.T, precision=HIGH)
    cross = jnp.dot(grads, test_grads.astype(F32).T, precision=HIGH)
    ndocs = gram.shape[0]
    damp = 0.1 * jnp.trace(gram) / ndocs
    factor = jnp.linalg.cholesky(gram / ndocs + damp * jnp.eye(ndocs, dtype=F32))
    middle = lax.linalg.triangular_solve(factor, cross, left_side=True, lower=True)
    solved = lax.linalg.triangular_solve(factor, middle, left_side=True, lower=True, transpose_a=True)
    placing = (doc_ids[None, :] == jnp.arange(ndocs, dtype=jnp.int32)[:, None]).astype(F32)
    return jnp.dot(placing, solved, precision=HIGH)


def place(seq, dp):
    bits = seq ^ (seq >> 1) ^ (seq >> 2) ^ (dp >> 1)
    return bits & 1


def here():
    seq, dp = lax.axis_index("seq"), lax.axis_index("dp")
    return seq, dp, place(seq, dp)


def in_vmem(*arrays):
    return [pltpu.with_memory_space_constraint(x, VMEM) for x in arrays]


def vmem_call(body, outs, args, hbm=(), scratch=(), name=None, moved=0):
    specs = [pl.BlockSpec(memory_space=VMEM)] * len(args) + [pl.BlockSpec(memory_space=pltpu.HBM)] * len(hbm)
    far = [pltpu.with_memory_space_constraint(x, pltpu.HBM) for x in hbm]
    return pl.pallas_call(
        body,
        out_shape=[VMEM(s, d) for s, d in outs],
        in_specs=specs,
        out_specs=[pl.BlockSpec(memory_space=VMEM)] * len(outs),
        scratch_shapes=list(scratch),
        name=name,
        compiler_params=pltpu.CompilerParams(vmem_limit_bytes=LIMIT),
        cost_estimate=pl.CostEstimate(flops=0, transcendentals=0, bytes_accessed=moved),
    )(*in_vmem(*args), *far)


def source(seq, slot):
    even, odd = ((0, 0), (5, 3), (3, 5), (6, 6))[slot]
    return seq ^ jnp.where(seq & 1 == 0, even, odd)


def weights_body(valid, blocks, out_t, in_t, first, second, whole, weights, valid_v, blocks_s, sems):
    seq, _, _ = here()
    rows_out, rows_in, size = out_t.shape[1], in_t.shape[1], first.shape[1]
    copies = [
        pltpu.make_async_copy(valid, valid_v, sems.at[0]),
        pltpu.make_async_copy(blocks, blocks_s, sems.at[1]),
        pltpu.make_async_copy(out_t, whole.at[:, pl.ds(0, rows_out)], sems.at[2]),
        pltpu.make_async_copy(in_t, whole.at[:, pl.ds(rows_out, rows_in)], sems.at[3]),
    ]
    for c in copies:
        c.start()
    for c in copies[:2]:
        c.wait()
    slots = valid.shape[1]
    blk = (seq * slots + lax.broadcasted_iota(jnp.int32, weights.shape, 1)) // BLOCK
    row = lax.broadcasted_iota(jnp.int32, weights.shape, 0)
    owner = jnp.zeros_like(blk)
    end = 0
    for j in range(blocks.shape[1]):
        end = end + blocks_s[0, j]
        owner = owner + (blk >= end).astype(jnp.int32)
    weights[...] = jnp.where((owner == row) & (valid_v[...] == 1), 1.0, 0.0)
    for c in copies[2:]:
        c.wait()
    first[...] = whole[:, :size]
    second[...] = whole[:, size:]


def column_copies(og, inp, three, last, mine, sems):
    nseq = lax.axis_size("seq")
    wo, wi = og.shape[1] // nseq, inp.shape[1] // nseq
    copies = []
    for k in range(4):
        shard = source(mine, k)
        out, base = (last, 0) if k == 3 else (three, k * (wo + wi))
        copies.append(pltpu.make_async_copy(
            og.at[:, pl.ds(pl.multiple_of(shard * wo, wo), wo)], out.at[:, pl.ds(base, wo)], sems.at[2 * k]))
        copies.append(pltpu.make_async_copy(
            inp.at[:, pl.ds(pl.multiple_of(shard * wi, wi), wi)], out.at[:, pl.ds(base + wo, wi)], sems.at[2 * k + 1]))
    return copies


def nt(a, b, precision=None):
    return lax.dot_general(a, b, (((1,), (1,)), ((), ())), precision=precision, preferred_element_type=F32)


def project(w, near, base, far, shard, width, skip):
    rows = w.shape[1]
    start = pl.multiple_of(shard * width + skip, 128)
    return nt(w, jnp.concatenate([near[:, pl.ds(base, rows)], far[:, pl.ds(start, rows)]], axis=0))


def keep_body(_, og, inp, tests, ids, near, late, t_own, t_far, rows, ids_s, sems):
    seq, _, half = here()
    hf = t_own.shape[1]
    copies = column_copies(og, inp, near, late, seq, sems)
    copies.append(pltpu.make_async_copy(tests.at[:, pl.ds(pl.multiple_of(half * hf, hf), hf)], t_own, sems.at[8]))
    copies.append(pltpu.make_async_copy(tests.at[:, pl.ds(pl.multiple_of((1 - half) * hf, hf), hf)], t_far, sems.at[9]))
    copies.append(pltpu.make_async_copy(ids, ids_s, sems.at[10]))
    for c in copies:
        c.start()
    for c in copies:
        c.wait()
    for r in range(rows.shape[0]):
        rows[r:r + 1, :] = jnp.full((1, rows.shape[1]), ids_s[r], jnp.int32)


def after_body(x, _, out):
    out[...] = x[...]


def near_body(own, a1, a2, b, og2, inp2, near, pg, px, *, wi, wo):
    seq, _, _ = here()
    size = a1.shape[1]
    rest = wo - size
    total, total_x = 0.0, 0.0
    for k, w in ((0, own), (2, b), (1, None)):
        base, shard = k * (wo + wi), source(seq, k)
        if w is None:
            total = total + project(a1[...], near, base, og2, shard, wo, 0)
            total = total + project(a2[:, :rest], near, base + size, og2, shard, wo, size)
            total_x = total_x + project(a2[:, rest:], near, base + wo, inp2, shard, wi, 0)
        else:
            total = total + project(w[:, :wo], near, base, og2, shard, wo, 0)
            total_x = total_x + project(w[:, wo:], near, base + wo, inp2, shard, wi, 0)
    pg[...] = total
    px[...] = total_x


def diagonal_body(c1, pg_in, near, og2, pg, *, wo):
    seq, _, _ = here()
    pg[...] = pg_in[...] + project(c1[...], near, 0, og2, source(seq, 3), wo, 0)


def last_body(c2, pg_in, px_in, near, og2, inp2, weights, out, *, wi, wo):
    seq, _, _ = here()
    rest = c2.shape[1] - wi
    rows = pg_in.shape[0]
    shard = source(seq, 3)
    out[:rows] = pg_in[...] + project(c2[:, :rest], near, wo - rest, og2, shard, wo, wo - rest)
    out[rows:2 * rows] = px_in[...] + project(c2[:, rest:], near, wo, inp2, shard, wi, 0)
    out[2 * rows:] = jnp.concatenate([weights[...], jnp.zeros_like(weights)], axis=1)


def halves(x):
    high = x.astype(jnp.bfloat16)
    return [high, (x - high.astype(F32)).astype(jnp.bfloat16)]


def grads_body(mine, far, grads, pgs):
    _, _, half = here()
    slots = pgs.shape[2]
    rows = (mine.shape[0] - 8) // 2
    hw = rows // 2
    pairs = hw // 2
    docs = grads.shape[0] // pairs
    both = []
    for base in (0, rows):
        block = pl.ds(base, rows)
        both.append([mine[block, :slots] + far[block, slots:], mine[block, slots:] + far[block, :slots]])
    for u in range(2):
        pgs[u] = jnp.where(half == 1, both[0][u][hw:], both[0][u][:hw])
    px = jnp.concatenate(both[1], axis=1)
    tokens = jnp.concatenate([mine[2 * rows:, :slots], far[2 * rows:, :slots]], axis=1)
    parts = []
    for q in range(2):
        some = jnp.concatenate([pgs[u, pl.ds(q, pairs, stride=2), :] for u in range(2)], axis=1)
        weighted = jnp.concatenate([some * tokens[j:j + 1, :] for j in range(docs)], axis=0)
        high, low = halves(weighted)
        px_high, px_low = halves(px)
        parts.append(nt(high, px_high) + (nt(high, px_low) + nt(low, px_high)))
    grads[...] = jnp.concatenate(parts, axis=1)


def sum_body(own, px, py, pd, out):
    out[...] = (own[...] + px[...]) + (py[...] + pd[...])


def products_body(m0, m3, m2, m1, t_own, t_far, out, every):
    seq, dp, _ = here()
    rows = m0.shape[0]
    for k, m in zip((0, 3, 2, 1), (m0, m3, m2, m1)):
        every[pl.ds(pl.multiple_of((dp ^ k) * rows, rows), rows), :] = m[...]
    docs = out.shape[0]
    pairs = every.shape[0] // docs
    flat = jnp.concatenate([every[pl.ds(i, docs, stride=pairs), :] for i in range(pairs)], axis=1)
    own, far = t_own[...], t_far[...]
    core = seq & 1
    high, low = halves(flat)
    ntest = 2 * own.shape[0]
    right = [jnp.where(core == 0, own, far), jnp.where(core == 0, far, own), high, low]
    both = nt(jnp.concatenate([high, low], axis=0), jnp.concatenate(right, axis=0))
    top, bottom = both[:docs], both[docs:]
    cross = top[:, :ntest] + bottom[:, :ntest]
    gram = top[:, ntest:ntest + docs] + (top[:, ntest + docs:] + bottom[:, ntest:ntest + docs])
    pad = jnp.zeros((docs, out.shape[1] - cross.shape[1] - docs), F32)
    out[...] = jnp.concatenate([cross, gram, pad], axis=1)


def solve_body(mine, far, rows, out):
    docs, tests = out.shape
    seq, _, _ = here()
    both = mine[...] + far[...]
    shape = both.shape
    row = lax.broadcasted_iota(jnp.int32, shape, 0)
    columns = [jnp.broadcast_to(both[:, 2 * tests + k:2 * tests + k + 1], shape) for k in range(docs)]
    trace = columns[0][0:1, :]
    for k in range(1, docs):
        trace = trace + columns[k][k:k + 1, :]
    damp = 0.1 * trace / docs
    columns = [c / docs + jnp.where(row == k, damp, 0.0) for k, c in enumerate(columns)]
    scale = jnp.zeros(shape, F32)
    for k in range(docs):
        inverse = 1.0 / columns[k][k:k + 1, :]
        scale = jnp.where(row == k, inverse, scale)
        factor = jnp.where(row == k, 0.0, columns[k] * inverse)
        both = both - factor * both[k:k + 1, :]
        for j in range(k + 1, docs):
            columns[j] = columns[j] - factor * columns[j][k:k + 1, :]
    solved = both * scale
    placed = jnp.zeros(shape, F32)
    for r in range(docs):
        placed = jnp.where(row == rows[r:r + 1, :], solved[r:r + 1, :], placed)
    out[...] = jnp.where(seq & 1 == 0, placed[:, :tests], placed[:, tests:2 * tests])


def paired_chips(inputs, out_grads, valid, doc_blocks, doc_ids, proj_in, proj_out, test_grads):
    ndp, nseq = lax.axis_size("dp"), lax.axis_size("seq")
    docs = doc_blocks.shape[1]
    ndocs = docs * ndp
    inp, og = inputs[0], out_grads[0]
    width = proj_out.shape[1]
    hw = width // 2
    wo, wi = proj_out.shape[0], proj_in.shape[0]
    slots = og.shape[0]
    ntest, feat = test_grads.shape
    bf = jnp.bfloat16

    def move(x, to):
        pairs = [(z * nseq + s, (lambda t: t[0] * nseq + t[1])(to(z, s))) for z in range(ndp) for s in range(nseq)]
        return lax.ppermute(x, ("dp", "seq"), pairs)

    def swap(x):
        return move(x, lambda z, s: (z, s ^ 1))

    def ring(x, step):
        return move(x, lambda z, s: (z, s ^ ((3, 5)[(s & 1) ^ step])))

    size = (wo + wi) * 5 // 8 // 128 * 128
    first, second, whole, weights = vmem_call(
        weights_body,
        [((width, size), bf), ((width, wo + wi - size), bf), ((width, wo + wi), bf), ((8, slots), F32)],
        [], hbm=[valid, doc_blocks, proj_out.T, proj_in.T],
        scratch=[VMEM((1, slots), jnp.int32), pltpu.SMEM((1, docs), jnp.int32), pltpu.SemaphoreType.DMA((4,))],
        name="weights",
    )
    a1, a2, b = ring(first, 0), ring(second, 0), ring(whole, 1)
    og2, inp2 = swap(og), swap(inp)
    lanes = -(-(2 * ntest + ndocs) // 128) * 128
    three, near, t_own, t_send, rows = vmem_call(
        keep_body,
        [((slots, 3 * (wo + wi)), bf), ((slots, wo + wi), bf)] + [((ntest, feat // 2), bf)] * 2 + [((ndocs, lanes), jnp.int32)],
        [whole], hbm=[og, inp, test_grads, doc_ids],
        scratch=[pltpu.SMEM((ndocs,), jnp.int32), pltpu.SemaphoreType.DMA((11,))], name="keep",
    )
    (a1,) = vmem_call(after_body, [(a1.shape, bf)], [a1, rows], name="after")
    c1 = ring(a1, 0)
    c2 = ring(a2, 0)
    part = ((width, 2 * slots), F32)
    pg, px = vmem_call(
        functools.partial(near_body, wi=wi, wo=wo), [part, part], [whole, a1, a2, b, og2, inp2, three], name="near",
    )
    (pg,) = vmem_call(functools.partial(diagonal_body, wo=wo), [part], [c1, pg, near, og2], name="diagonal")
    (mine,) = vmem_call(
        functools.partial(last_body, wi=wi, wo=wo), [((2 * width + 8, 2 * slots), F32)],
        [c2, pg, px, near, og2, inp2, weights], name="last",
    )
    pairs = hw // 2
    (grads,) = vmem_call(
        grads_body, [((docs * pairs, 2 * width), F32)], [mine, swap(mine)],
        scratch=[VMEM((2, hw, slots), F32)], name="grads",
    )
    px = move(grads, lambda z, s: (z, s ^ 3))
    py = move(grads, lambda z, s: (z, s ^ 5))
    pd = move(grads, lambda z, s: (z, s ^ 6))
    grads = (grads + px) + (py + pd)
    m3 = move(grads, lambda z, s: (z ^ 3, s ^ 1))
    m2 = move(grads, lambda z, s: (z ^ 2, s ^ 1))
    m1 = move(grads, lambda z, s: (z ^ 1, s))
    t_far = swap(t_send)
    (mine,) = vmem_call(
        products_body, [((ndocs, lanes), F32)],
        [grads, m3, m2, m1, t_own, t_far],
        scratch=[VMEM((ndp * docs * pairs, 2 * width), F32)], name="products",
    )
    return pl.pallas_call(
        solve_body,
        out_shape=jax.ShapeDtypeStruct((ndocs, ntest), F32),
        in_specs=[pl.BlockSpec(memory_space=VMEM)] * 3,
        out_specs=pl.BlockSpec(memory_space=VMEM),
        name="solve",
    )(*in_vmem(mine, swap(mine), rows))


def solution(mesh):
    in_specs = (
        P("dp", "seq", None),
        P("dp", "seq", None),
        P("dp", "seq"),
        P("dp", None),
        P(),
        P("seq", None),
        P("seq", None),
        P("seq", None),
    )
    fast = mesh.shape["seq"] == 8 and mesh.shape["dp"] == 4
    return jax.shard_map(
        paired_chips if fast else any_mesh,
        mesh=mesh, in_specs=in_specs, out_specs=P(None, "seq"), check_vma=False,
    )
```
